256 devices in a mesh: freq: 16 (over y, x), stn: 16 (over z, core).
Axes of the slice: x: 4, y: 4, z: 8, core: 2. Of those that a mesh axis runs over, the one named last changes fastest.
Arguments:
- visibilities: float32 [16, 8, 1024, 1024], P('freq', None, 'stn'), may hold values from -6 to 6
- flag_mask: int32 [1024, 1024], P('stn'), may hold values 0 or 1
- stations: float32 [3, 1024], P(None, 'stn'), may hold values from -32 to 32
- directions: float32 [2, 1536], replicated, may hold values from -0.5 to 0.5
- intensity: float32 [1536], replicated, may hold values from 0.02 to 0.2
- polarized: float32 [2, 1536], replicated, may hold values from -0.4375 to 0.4375
- spectral: float32 [1536], replicated, may hold values from -1.5 to 0.5
- clusters: int32 [1536], replicated, may hold values from 0 to 15, as said below
- jones_gains: float32 [16, 8, 16, 1024], P('freq', None, None, 'stn'), may hold values from -6 to 6
- scaled_duals: float32 [16, 8, 16, 1024], P('freq', None, None, 'stn'), may hold values from -4 to 4
- consensus: float32 [4, 8, 16, 1024], P(None, None, None, 'stn'), may hold values from -6 to 6
Outputs:
- jones_next: float32 [16, 8, 16, 1024], P('freq', None, None, 'stn')
- duals_next: float32 [16, 8, 16, 1024], P('freq', None, None, 'stn')
- consensus_next: float32 [4, 8, 16, 1024], P(None, None, None, 'stn')
The draws below stay inside these ranges and needn't reach their ends.
Inputs may be any that keep to these rules, and one draw needn't show every extreme that they name: `clusters`: every direction holds exactly 96 components.
All inputs are finite; a program needn't handle non-finite values. No bound on the sum of `flag_mask` on one device may be relied on, other than what follows from the above.
Results may differ from the reference program's by a relative error of at most 0.0019.
Values may be sent and summed in bfloat16 or wider, within the bound.
No kernel may reach another device: no remote copies, remote signals or barrier semaphores. Data moves between devices by JAX's collectives and lax.ppermute only.
A program may use at most 64 MiB of HBM per device.

```python
import math
import jax
import jax.numpy as jnp
from jax import lax

DIRS = 16
COMPS = 1536
POLY = 4
NS = 1024
FREQS = 16


def draw_clusters(key, part):
    key = jax.random.fold_in(key, 7)
    return (jax.random.permutation(key, COMPS) % DIRS).astype(jnp.int32)


def plant(values, own_key, low, largest):
    longest = values.shape.index(max(values.shape))
    spots = []
    for shift in (0, 1):
        where = [jax.random.randint(jax.random.fold_in(own_key, axis), (), 0, length) for axis, length in enumerate(values.shape)]
        where[longest] = (where[longest] + shift) % values.shape[longest]
        spots.append(tuple(where))
    return values.at[spots[0]].set(low).at[spots[1]].set(largest)


def steps_of(own_key, dims, shards, least, largest):
    level = 1.0
    for dim, blocks in shards:
        steps = jax.random.uniform(jax.random.fold_in(jax.random.fold_in(own_key, 6), dim), (blocks,), jnp.float32, least / len(shards), largest / len(shards))
        level = level * jnp.repeat(jnp.exp(steps), dims[dim] // blocks).reshape((-1,) + (1,) * (len(dims) - 1 - dim))
    return level


def gaussian(rng, extent, scale, bound, shards=(), held_as=jnp.bfloat16):
    values = jax.random.normal(rng, extent, jnp.float32) * scale
    if len(shards) > 0:
        values = steps_of(rng, extent, shards, -0.22, 0.18) * values
    return jnp.clip(values, min=-bound, max=bound).astype(held_as)


def setup_inputs(seed: int = 0) -> dict:
    key_of = jax.random.split(jax.random.key(seed), 12)
    return {
        "visibilities": gaussian(key_of[0], (FREQS, 8, NS, NS), 1.0, 6.0, ((0, 16), (2, 16)), jnp.float32),
        "flag_mask": plant((jax.random.randint(key_of[1], (NS, NS), 0, 8) < 7).astype(jnp.int32), jax.random.fold_in(key_of[1], 1), 0, 1),
        "stations": gaussian(key_of[2], (3, NS), 5.0, 32.0, ((1, 16),), jnp.float32),
        "directions": jnp.clip(jax.random.uniform(key_of[3], (2, COMPS), jnp.float32, -0.5, 0.5), -0.5, 0.5),
        "intensity": jnp.clip(jnp.exp(jax.random.uniform(key_of[4], (COMPS,), jnp.float32, math.log(0.02), math.log(0.2))), 0.02, 0.2),
        "polarized": gaussian(key_of[5], (2, COMPS), 0.03, 0.4375, (), jnp.float32),
        "spectral": jnp.clip(jax.random.uniform(key_of[6], (COMPS,), jnp.float32, -1.5, 0.5), -1.5, 0.5),
        "clusters": draw_clusters(jax.random.fold_in(key_of[11], 71), 0),
        "jones_gains": gaussian(key_of[8], (FREQS, 8, DIRS, NS), 0.7, 6.0, ((0, 16), (3, 16)), jnp.float32),
        "scaled_duals": gaussian(key_of[9], (FREQS, 8, DIRS, NS), 0.3, 4.0, ((0, 16), (3, 16)), jnp.float32),
        "consensus": gaussian(key_of[10], (POLY, 8, DIRS, NS), 0.4, 6.0, ((3, 16),), jnp.float32),
    }


TWO_PI = 6.283185307179586
PENALTY = 40.0
STEP_SIZE = 0.5

def complex_mul(lhs_value, rhs_value):
    return (lhs_value[0] * rhs_value[0] - lhs_value[1] * rhs_value[1], lhs_value[0] * rhs_value[1] + lhs_value[1] * rhs_value[0])

def complex_add(lhs_value, rhs_value):
    return (lhs_value[0] + rhs_value[0], lhs_value[1] + rhs_value[1])

def complex_conj(number):
    return (number[0], -number[1])

def matrix_mul(lhs_matrix, rhs_matrix):
    return [complex_add(complex_mul(lhs_matrix[0], rhs_matrix[0]), complex_mul(lhs_matrix[1], rhs_matrix[2])), complex_add(complex_mul(lhs_matrix[0], rhs_matrix[1]), complex_mul(lhs_matrix[1], rhs_matrix[3])), complex_add(complex_mul(lhs_matrix[2], rhs_matrix[0]), complex_mul(lhs_matrix[3], rhs_matrix[2])), complex_add(complex_mul(lhs_matrix[2], rhs_matrix[1]), complex_mul(lhs_matrix[3], rhs_matrix[3]))]

def matrix_herm(matrix):
    return [complex_conj(matrix[0]), complex_conj(matrix[2]), complex_conj(matrix[1]), complex_conj(matrix[3])]

def unpack_matrix(stacked):
    return [(stacked[0], stacked[1]), (stacked[2], stacked[3]), (stacked[4], stacked[5]), (stacked[6], stacked[7])]

def pack_matrix(matrix):
    return jnp.stack([member for element in matrix for member in element])

def summed_pack(matrix, reduce_dim):
    return -jnp.stack([lax.optimization_barrier(jnp.sum(member, reduce_dim)) for element in matrix for member in element])

def band_ratio(index_value, band_count):
    return 0.5 + 3.0 * (index_value.astype(jnp.float32) + 0.5) / band_count

def phase_table(positions, sky_dirs, freq_ratio):
    dir_l = sky_dirs[0][:, None]
    dir_m = sky_dirs[1][:, None]
    dir_n = jnp.sqrt(1.0 - dir_l * dir_l - dir_m * dir_m)
    geometry = dir_l * positions[0][None, :] + dir_m * positions[1][None, :] + (dir_n - 1.0) * positions[2][None, :]
    phase_angle = TWO_PI * freq_ratio * geometry
    return jnp.stack([jnp.cos(phase_angle), -jnp.sin(phase_angle)]).astype(jnp.bfloat16)

def flux_weights(intensity, polarized, spectral, freq_ratio):
    factor = jnp.power(freq_ratio, spectral)
    return jnp.stack([(intensity + polarized[0]) * factor, polarized[1] * factor, (intensity - polarized[0]) * factor])

def legendre_table(band_count):
    centre = (2.0 * jnp.arange(band_count, dtype=jnp.float32) + 1.0) / band_count - 1.0
    return jnp.stack([jnp.ones_like(centre), centre, 0.5 * (3.0 * centre * centre - 1.0), 0.5 * (5.0 * centre * centre * centre - 3.0 * centre)], axis=1)

def gram_solve(gram_matrix, rhs_rows):
    chol_lower = jnp.linalg.cholesky(gram_matrix)
    forward = []
    for row_at in range(4):
        current = rhs_rows[row_at]
        for col_at in range(row_at):
            current = current - chol_lower[row_at, col_at] * forward[col_at]
        forward.append(current / chol_lower[row_at, row_at])
    backward = [forward[0]] * 4
    for row_at in (3, 2, 1, 0):
        current = forward[row_at]
        for col_at in range(row_at + 1, 4):
            current = current - chol_lower[col_at, row_at] * backward[col_at]
        backward[row_at] = current / chol_lower[row_at, row_at]
    return jnp.stack(backward)

def coherence(direction, own_table, all_table, weights, block_span):
    offset = direction * block_span
    own_real = lax.dynamic_slice_in_dim(own_table[0], offset, block_span, 0)
    own_imag = lax.dynamic_slice_in_dim(own_table[1], offset, block_span, 0)
    weight_block = lax.dynamic_slice_in_dim(weights, offset, block_span, 1)
    blocks = []
    for flux_at in range(3):
        factor_col = weight_block[flux_at][:, None]
        blocks.append(jnp.concatenate([own_real * factor_col, own_imag * factor_col], 0).astype(jnp.bfloat16))
    operand_left = jnp.concatenate(blocks, 1)
    far_real = lax.dynamic_slice_in_dim(all_table[0], offset, block_span, 0)
    far_imag = lax.dynamic_slice_in_dim(all_table[1], offset, block_span, 0)
    operand_right = jnp.concatenate([jnp.concatenate([far_real, -far_imag], 1), jnp.concatenate([far_imag, far_real], 1)], 0)
    product = lax.dot_general(operand_left.astype(jnp.float32), operand_right.astype(jnp.float32), (((0,), (0,)), ((), ())), precision=lax.Precision.HIGHEST, preferred_element_type=jnp.float32)
    row_count = own_real.shape[1]
    col_count = far_real.shape[1]
    entries = [(product[flux_at * row_count:(flux_at + 1) * row_count, :col_count], product[flux_at * row_count:(flux_at + 1) * row_count, col_count:]) for flux_at in range(3)]
    return [entries[0], entries[1], entries[1], entries[2]]

def residual_of(band_vis, mask_float, near_gains, far_gains, own_table, all_table, weights, block_span):

    def direction_step(model_sum, direction):
        coh_matrix = coherence(direction, own_table, all_table, weights, block_span)
        near_jones = unpack_matrix(lax.dynamic_index_in_dim(near_gains, direction, 1, keepdims=False)[:, :, None])
        far_jones = unpack_matrix(lax.dynamic_index_in_dim(far_gains, direction, 1, keepdims=False)[:, None, :])
        model_term = matrix_mul(matrix_mul(near_jones, coh_matrix), matrix_herm(far_jones))
        return (model_sum + pack_matrix(model_term), None)
    model_sum, _ = lax.scan(direction_step, jnp.zeros(band_vis.shape, jnp.float32), jnp.arange(near_gains.shape[1], dtype=jnp.int32))
    return (band_vis - model_sum) * mask_float[None]

def gradient_of(residual, near_gains, far_gains, own_table, all_table, weights, block_span):
    res_matrix = unpack_matrix(residual)

    def direction_step(state_value, direction):
        coh_matrix = coherence(direction, own_table, all_table, weights, block_span)
        near_jones = unpack_matrix(lax.dynamic_index_in_dim(near_gains, direction, 1, keepdims=False)[:, :, None])
        far_jones = unpack_matrix(lax.dynamic_index_in_dim(far_gains, direction, 1, keepdims=False)[:, None, :])
        col_part = matrix_mul(matrix_herm(res_matrix), matrix_mul(near_jones, coh_matrix))
        row_part = matrix_mul(res_matrix, matrix_mul(far_jones, matrix_herm(coh_matrix)))
        return (state_value, (summed_pack(row_part, 1), summed_pack(col_part, 0)))
    _, (row_terms, col_terms) = lax.scan(direction_step, jnp.zeros((), jnp.float32), jnp.arange(near_gains.shape[1], dtype=jnp.int32))
    return (row_terms, col_terms)

def reference(visibilities, flag_mask, stations, directions, intensity, polarized, spectral, clusters, jones_gains, scaled_duals, consensus):
    sort_order = jnp.argsort(clusters, stable=True)
    sky_dirs = directions[:, sort_order]
    sky_flux = intensity[sort_order]
    sky_pol = polarized[:, sort_order]
    sky_index = spectral[sort_order]
    block_span = COMPS // DIRS
    mask_float = flag_mask.astype(jnp.float32)
    basis_table = legendre_table(FREQS)

    def one_band(band_item):
        band_index, band_vis, band_jones, band_duals, basis_row = band_item
        freq_ratio = band_ratio(band_index, FREQS)
        phase_tab = phase_table(stations, sky_dirs, freq_ratio)
        weights = flux_weights(sky_flux, sky_pol, sky_index, freq_ratio)
        residual = residual_of(band_vis, mask_float, band_jones, band_jones, phase_tab, phase_tab, weights, block_span)
        row_terms, col_terms = gradient_of(residual, band_jones, band_jones, phase_tab, phase_tab, weights, block_span)
        poly_value = lax.optimization_barrier(jnp.sum(basis_row[:, None, None, None] * consensus, 0))
        drive = jnp.transpose(row_terms + col_terms, (1, 0, 2)) + PENALTY / 2.0 * (band_jones - poly_value + band_duals)
        step_length = STEP_SIZE / jnp.sqrt(jnp.sum(drive * drive) / drive.size + 1e-06)
        return band_jones - step_length * drive
    jones_next = lax.map(one_band, (jnp.arange(FREQS, dtype=jnp.int32), visibilities, jones_gains, scaled_duals, basis_table))
    summed = jnp.einsum('fi,fckn->ickn', basis_table, jones_next + scaled_duals, precision=lax.Precision.HIGHEST)
    gram_matrix = jnp.dot(basis_table.T, basis_table, precision=lax.Precision.HIGHEST)
    consensus_next = gram_solve(gram_matrix, summed.reshape(4, -1)).reshape(summed.shape)
    poly_next = jnp.einsum('fi,ickn->fckn', basis_table, consensus_next, precision=lax.Precision.HIGHEST)
    duals_next = scaled_duals + jones_next - poly_next
    return (jones_next, duals_next, consensus_next)
```

```python
import math

import jax
import jax.numpy as jnp
import numpy as np
from jax import lax
from jax.experimental import pallas as pl
from jax.experimental.pallas import tpu as pltpu
from jax.sharding import PartitionSpec as P

DIRS = 16
COMPS = 1536
BANDS = 16
BLOCKS = 16
NS = 1024
OWN = 64
ENTRIES = 131072
PENALTY = 40.0
STEP_SIZE = 0.5
F32 = jnp.float32
BF16 = jnp.bfloat16
SPAN = 128
STEPS = COMPS // SPAN
VMEM = pl.BlockSpec(memory_space=pltpu.VMEM)
SMEM = pl.BlockSpec(memory_space=pltpu.SMEM)


def turn_polynomials():
    nodes = (np.cos(np.pi * (np.arange(64) + 0.5) / 64) + 1.0) / 8.0
    root = np.sqrt(nodes)
    cos_fit = np.polynomial.Chebyshev.fit(nodes, np.cos(2 * np.pi * root), 6, domain=[0, 0.25])
    sin_fit = np.polynomial.Chebyshev.fit(
        nodes, -np.sin(2 * np.pi * root) / root, 5, domain=[0, 0.25]
    )
    to_list = lambda fit: [float(v) for v in fit.convert(kind=np.polynomial.Polynomial).coef]
    return to_list(cos_fit), to_list(sin_fit)


COS_POLY, SIN_POLY = turn_polynomials()


def legendre_rows():
    centre = (2.0 * np.arange(BANDS) + 1.0) / BANDS - 1.0
    return np.stack(
        [
            np.ones_like(centre),
            centre,
            0.5 * (3.0 * centre * centre - 1.0),
            0.5 * (5.0 * centre * centre * centre - 3.0 * centre),
        ],
        axis=1,
    )


def horner(coefs, value):
    total = coefs[-1]
    for coef in coefs[-2::-1]:
        total = total * value + coef
    return total


def phases(turns):
    frac = turns - jnp.floor(turns + 0.5)
    square = frac * frac
    real = horner(COS_POLY, square)
    imag = frac * horner(SIN_POLY, square)
    return real.astype(BF16).astype(F32), imag.astype(BF16).astype(F32)


def split3(value):
    high = value.astype(BF16).astype(F32)
    rest = value - high
    middle = rest.astype(BF16).astype(F32)
    return high, middle, (rest - middle).astype(BF16).astype(F32)


def band_basis(band):
    centre = (2.0 * band.astype(F32) + 1.0) / BANDS - 1.0
    return (
        jnp.float32(1.0),
        centre,
        0.5 * (3.0 * centre * centre - 1.0),
        0.5 * (5.0 * centre * centre * centre - 3.0 * centre),
    )


def gains_rows(ref, lead=()):
    groups = []
    for column in range(2):
        for part in range(2):
            at = 2 * column + part
            groups.append(jnp.concatenate([ref[lead + (at,)], ref[lead + (4 + at,)]], axis=1))
    return jnp.concatenate(groups, axis=0)


def put_gains(ref, rows, lead=()):
    for column in range(2):
        for part in range(2):
            at = 2 * column + part
            group = rows[at * 16 : at * 16 + 16]
            ref[lead + (at,)] = group[:, :64]
            ref[lead + (4 + at,)] = group[:, 64:]


def packet_kernel(jones_ref, stations_ref, own_ref, copies_ref):
    place = jnp.concatenate([stations_ref[...], stations_ref[...]], axis=1)
    rows = jnp.concatenate([gains_rows(jones_ref), place, jnp.zeros((5, 128), F32)], axis=0)
    own_ref[...] = rows
    copies_ref[...] = jnp.broadcast_to(rows[None], copies_ref.shape)


def prepare_kernel(
    band_ref,
    vis_ref,
    mask_ref,
    dirs_ref,
    flux_ref,
    pol_ref,
    index_ref,
    clusters_ref,
    out_ref,
    sky_ref,
):
    @pl.when(pl.program_id(0) == 0)
    def _():
        prepare_sky(band_ref, dirs_ref, flux_ref, pol_ref, index_ref, clusters_ref, sky_ref)

    mask = mask_ref[...].astype(F32)

    def put(pair, real, imag):
        turned = jnp.concatenate([real, imag], axis=0).T.astype(BF16)
        for dest in range(2):
            out_ref[dest, pair * 64 : pair * 64 + 64, :] = turned[dest * 64 : dest * 64 + 64]

    for pair in range(4):
        put(pair, vis_ref[2 * pair] * mask, vis_ref[2 * pair + 1] * mask)
    put(4, mask, mask)


def flat(ref):
    return jnp.concatenate([ref[at : at + 1, :] for at in range(COMPS // 128)], axis=1)


def prepare_sky(band_ref, dirs_ref, flux_ref, pol_ref, index_ref, clusters_ref, out_ref):
    ratio = 0.5 + 3.0 * (band_ref[0].astype(F32) + 0.5) / BANDS
    dir_l = dirs_ref[0:1, :]
    dir_m = dirs_ref[1:2, :]
    dir_n = jnp.sqrt(1.0 - dir_l * dir_l - dir_m * dir_m) - 1.0
    log_ratio = jnp.log(jnp.full((1, COMPS), ratio, F32))
    factor = jnp.exp(flat(index_ref) * log_ratio)
    flux = flat(flux_ref)
    stokes_q = pol_ref[0:1, :]
    rows = [
        dir_l * ratio,
        dir_m * ratio,
        dir_n * ratio,
        (flux + stokes_q) * factor,
        pol_ref[1:2, :] * factor,
        (flux - stokes_q) * factor,
    ]
    row_at = lax.broadcasted_iota(jnp.int32, (8, COMPS), 0)
    stacked = jnp.zeros((8, COMPS), F32)
    for at, row in enumerate(rows):
        stacked = jnp.where(row_at == at, row, stacked)
    high, middle, low = split3(stacked)
    table = jnp.concatenate(
        [high, high, high, middle, middle, low, jnp.zeros((80, COMPS), F32)], axis=0
    ).astype(BF16)
    clusters = flat(clusters_ref)
    hot = (lax.broadcasted_iota(jnp.int32, (16, COMPS), 0) == clusters).astype(F32)
    before = (
        lax.broadcasted_iota(jnp.int32, (128, 128), 0)
        < lax.broadcasted_iota(jnp.int32, (128, 128), 1)
    ).astype(BF16)
    seen = jnp.zeros((16, 1), F32)
    ranks = []
    for at in range(COMPS // 128):
        part = hot[:, at * 128 : at * 128 + 128]
        inside = jnp.dot(part.astype(BF16), before, preferred_element_type=F32) + seen
        ranks.append(jnp.sum(inside * part, axis=0, keepdims=True))
        seen = seen + jnp.sum(part, axis=1, keepdims=True)
    place = 16 * jnp.concatenate(ranks, axis=1).astype(jnp.int32) + clusters
    for at in range(COMPS // 256):
        target = lax.broadcasted_iota(jnp.int32, (256, COMPS), 0) + at * 256
        chosen = (target == place).astype(F32).astype(BF16)
        out_ref[at * 256 : at * 256 + 256, :] = lax.dot_general(
            chosen, table, (((1,), (1,)), ((), ())), preferred_element_type=F32
        ).astype(BF16)


def station_operand(rows8):
    high, middle, low = split3(rows8)
    width = rows8.shape[1]
    return jnp.concatenate(
        [high, middle, low, high, middle, high, jnp.zeros((80, width), F32)], axis=0
    ).astype(BF16)


def model_kernel(
    sky_ref, all_ref, own_ref, far_ref, weighted_ref, model_ref, geo_ref, geo_own_ref, gains_ref, turns_ref
):
    step = pl.program_id(0)
    lower = lax.broadcasted_iota(jnp.int32, (1, 128), 1) < 64

    @pl.when(step == 0)
    def _():
        model_ref[...] = jnp.zeros_like(model_ref)
        geo_own_ref[...] = station_operand(own_ref[64:72, :])
        for tile in range(8):
            first, second = all_ref[2 * tile], all_ref[2 * tile + 1]
            lanes = slice(tile * 128, tile * 128 + 128)
            geo_ref[:, lanes] = station_operand(jnp.where(lower, first[64:72], second[64:72]))
            low_part = jnp.where(lower, first[0:64], pltpu.roll(second[0:64], 64, 1))
            high_part = jnp.where(lower, pltpu.roll(first[0:64], 64, 1), second[0:64])
            gains_ref[:, lanes] = low_part
            gains_ref[:, 1024 + tile * 128 : 1024 + tile * 128 + 128] = high_part

    sky = sky_ref[...]
    turns_ref[...] = jnp.dot(sky, geo_ref[...], preferred_element_type=F32)

    def rows_step(at, carry):
        rows = pl.ds(pl.multiple_of(at * 16, 16), 16)
        for lane in range(0, NS, 256):
            real, imag = phases(turns_ref[rows, lane : lane + 256])
            for row in range(2):
                lanes = slice(row * NS + lane, row * NS + lane + 256)
                for column in range(2):
                    gain_re = gains_ref[column * 32 : column * 32 + 16, lanes]
                    gain_im = gains_ref[column * 32 + 16 : column * 32 + 32, lanes]
                    far_ref[column, rows, lanes] = (real * gain_re - imag * gain_im).astype(BF16)
                    far_ref[2 + column, rows, lanes] = (real * gain_im + imag * gain_re).astype(
                        BF16
                    )
        return carry

    lax.fori_loop(0, SPAN // 16, rows_step, 0)

    own_re, own_im = phases(jnp.dot(sky, geo_own_ref[...], preferred_element_type=F32))
    source = lax.broadcasted_iota(jnp.int32, (128, 384), 0)
    target = 3 + lax.broadcasted_iota(jnp.int32, (128, 384), 1) // 128
    select = (source == target) | (source == target + 24) | (source == target + 40)
    weights = jnp.dot(sky, select.astype(F32).astype(BF16), preferred_element_type=F32)
    weighted = []
    for flux in range(3):
        weight = weights[:, flux * 128 : flux * 128 + 128]
        pair = ((own_re * weight).astype(BF16), (own_im * weight).astype(BF16))
        weighted_ref[2 * flux] = pair[0]
        weighted_ref[2 * flux + 1] = pair[1]
        weighted.append((pair[0].astype(F32), pair[1].astype(F32)))
    gains = [jnp.concatenate([own_ref[at * 16 : at * 16 + 16]] * 8, axis=0) for at in range(4)]
    near_re, near_im = [], []
    for first, second in ((0, 1), (1, 2)):
        (ar, ai), (br, bi) = weighted[first], weighted[second]
        real = gains[0] * ar - gains[1] * ai + gains[2] * br - gains[3] * bi
        imag = gains[0] * ai + gains[1] * ar + gains[2] * bi + gains[3] * br
        near_re.append(real.T)
        near_im.append(imag.T)
    near = jnp.concatenate(
        [
            jnp.concatenate(near_re + near_im, axis=1),
            jnp.concatenate(near_im + [-near_re[0], -near_re[1]], axis=1),
        ],
        axis=0,
    ).astype(BF16)
    far = far_ref[...].reshape(4 * SPAN, 2 * NS)
    model_ref[...] += jnp.dot(near, far, preferred_element_type=F32)


def gradient_kernel(
    band_ref,
    block_ref,
    far_ref,
    weighted_ref,
    vis_ref,
    mask_ref,
    got_ref,
    model_ref,
    own_ref,
    duals_ref,
    consensus_ref,
    drive_ref,
    square_ref,
    both_ref,
    near_ref,
    sum_ref,
):
    step = pl.program_id(0)
    own_tile = block_ref[0] // 2

    @pl.when(step == 0)
    def _():
        sum_ref[...] = jnp.zeros_like(sum_ref)
        lower = lax.broadcasted_iota(jnp.int32, (1, 128), 1) < 64
        for tile in range(8):
            lanes = slice(tile * 128, tile * 128 + 128)
            mask = mask_ref[:, lanes].astype(F32)

            def halves(pair):
                first = got_ref[2 * tile, pair * 64 : pair * 64 + 64, :].astype(F32)
                second = got_ref[2 * tile + 1, pair * 64 : pair * 64 + 64, :].astype(F32)
                return first, second

            first, second = halves(4)
            mask_both = mask + jnp.where(lower, first, second)
            for row in range(2):
                for column in range(2):
                    first, second = halves(2 * column + row)
                    real = jnp.where(lower, first, pltpu.roll(second, 64, 1))
                    imag = jnp.where(lower, pltpu.roll(first, 64, 1), second)
                    at = column * NS + tile * 128
                    for part, other in ((0, real), (1, -imag)):
                        top = part * 128 + row * 64
                        vis = vis_ref[4 * row + 2 * column + part, :, lanes]
                        model = model_ref[top : top + 64, at : at + 128]
                        value = vis * mask + other - mask_both * model
                        high = value.astype(BF16)
                        both_ref[top : top + 64, at : at + 128] = high

                        @pl.when(tile == own_tile)
                        def _(value=value, high=high, top=top, column=column):
                            near_ref[top : top + 64, column * 128 : column * 128 + 128] = (
                                value - high.astype(F32)
                            ).astype(BF16)

    product = lax.dot_general(
        far_ref[...].reshape(4 * SPAN, 2 * NS),
        both_ref[...],
        (((1,), (1,)), ((), ())),
        preferred_element_type=F32,
    )
    lane = pl.multiple_of(own_tile * 128, 128)
    beside = jnp.concatenate(
        [
            far_ref[:, :, pl.ds(lane, 128)].reshape(4 * SPAN, 128),
            far_ref[:, :, pl.ds(NS + lane, 128)].reshape(4 * SPAN, 128),
        ],
        axis=1,
    )
    product = product + lax.dot_general(
        beside, near_ref[...], (((1,), (1,)), ((), ())), preferred_element_type=F32
    )
    terms = []
    for column in range(2):
        real_rows = product[column * SPAN : column * SPAN + SPAN]
        imag_rows = product[(2 + column) * SPAN : (2 + column) * SPAN + SPAN]
        terms.append(
            (
                real_rows[:, :128] - imag_rows[:, 128:],
                imag_rows[:, :128] + real_rows[:, 128:],
            )
        )
    weighted = [weighted_ref[at].astype(F32) for at in range(6)]
    for column, (first, second) in enumerate(((0, 1), (1, 2))):
        real = jnp.zeros((SPAN, 128), F32)
        imag = jnp.zeros((SPAN, 128), F32)
        for (tr, ti), flux in zip(terms, (first, second)):
            wr, wi = weighted[2 * flux], weighted[2 * flux + 1]
            real = real + (tr * wr + ti * wi)
            imag = imag + (ti * wr - tr * wi)
        for part, value in enumerate((real, imag)):
            at = (2 * column + part) * 16
            sum_ref[at : at + 16] += jnp.sum(value.reshape(SPAN // 16, 16, 128), axis=0)

    @pl.when(step == STEPS - 1)
    def _():
        basis = band_basis(band_ref[0])
        poly = jnp.zeros((64, 128), F32)
        for at in range(4):
            poly = poly + basis[at] * gains_rows(consensus_ref, (at,))
        penalty = PENALTY / 2.0 * (own_ref[0:64, :] - poly + gains_rows(duals_ref))
        drive = penalty - sum_ref[...]
        drive_ref[...] = drive
        square_ref[...] = jnp.broadcast_to(
            jnp.sum(drive * drive, axis=0, keepdims=True), square_ref.shape
        )


def update_kernel(squares_ref, drive_ref, own_ref, duals_ref, next_ref, shared_ref):
    total = jnp.sum(squares_ref[...], axis=(0, 1), keepdims=True)
    length = STEP_SIZE / jnp.sqrt(total / ENTRIES + 1e-6)
    rows = own_ref[0:64, :] - length * drive_ref[...]
    put_gains(next_ref, rows)
    shared_ref[...] = jnp.broadcast_to((rows + gains_rows(duals_ref))[None], shared_ref.shape)


def finish_kernel(band_ref, shared_ref, own_ref, duals_ref, consensus_ref):
    table = legendre_rows()
    gram = table.T @ table
    lower = np.linalg.cholesky(gram)
    sums = []
    for at in range(4):
        total = shared_ref[0] * float(table[0, at])
        for band in range(1, BANDS):
            total = total + shared_ref[band] * float(table[band, at])
        sums.append(total)
    forward = []
    for row in range(4):
        current = sums[row]
        for col in range(row):
            current = current - float(lower[row, col]) * forward[col]
        forward.append(current * float(1.0 / lower[row, row]))
    backward = [None] * 4
    for row in (3, 2, 1, 0):
        current = forward[row]
        for col in range(row + 1, 4):
            current = current - float(lower[col, row]) * backward[col]
        backward[row] = current * float(1.0 / lower[row, row])
    basis = band_basis(band_ref[0])
    poly = jnp.zeros((64, 128), F32)
    for at in range(4):
        put_gains(consensus_ref, backward[at], (at,))
        poly = poly + basis[at] * backward[at]
    put_gains(duals_ref, own_ref[0] - poly)


def cost(flops, moved):
    return pl.CostEstimate(flops=int(flops), bytes_accessed=int(moved), transcendentals=0)


def local(
    visibilities,
    flag_mask,
    stations,
    directions,
    intensity,
    polarized,
    spectral,
    clusters,
    jones_gains,
    scaled_duals,
    consensus,
):
    band = lax.axis_index("freq").reshape(1).astype(jnp.int32)
    block = lax.axis_index("stn").reshape(1).astype(jnp.int32)
    vis, jones, duals = visibilities[0], jones_gains[0], scaled_duals[0]
    shape = jax.ShapeDtypeStruct
    big = pltpu.CompilerParams(vmem_limit_bytes=56 * 1024 * 1024)
    own, copies = pl.pallas_call(
        packet_kernel,
        out_shape=[shape((72, 128), F32), shape((BLOCKS, 72, 128), F32)],
        in_specs=[VMEM] * 2,
        out_specs=[VMEM, VMEM],
        name="packet",
    )(jones, stations)
    everyone = lax.all_to_all(copies, "stn", 0, 0, tiled=True)
    outgoing, sky = pl.pallas_call(
        prepare_kernel,
        grid=(8,),
        in_specs=[
            SMEM,
            pl.BlockSpec((8, OWN, 128), lambda at: (0, 0, at)),
            pl.BlockSpec((OWN, 128), lambda at: (0, at)),
        ]
        + [VMEM] * 5,
        out_specs=[pl.BlockSpec((2, 320, 128), lambda at: (at, 0, 0)), VMEM],
        out_shape=[shape((BLOCKS, 320, 128), BF16), shape((COMPS, 128), BF16)],
        compiler_params=big,
        cost_estimate=cost(4e9, 1e6),
        name="prepare",
    )(
        band,
        vis,
        flag_mask,
        directions,
        intensity.reshape(COMPS // 128, 128),
        polarized,
        spectral.reshape(COMPS // 128, 128),
        clusters.reshape(COMPS // 128, 128),
    )
    incoming = lax.all_to_all(outgoing, "stn", 0, 0, tiled=True)
    far, weighted, model = pl.pallas_call(
        model_kernel,
        grid=(STEPS,),
        in_specs=[
            pl.BlockSpec((SPAN, 128), lambda at: (at, 0)),
            VMEM,
            VMEM,
        ],
        out_specs=[
            pl.BlockSpec((4, SPAN, 2 * NS), lambda at: (0, at, 0)),
            pl.BlockSpec((6, SPAN, 128), lambda at: (0, at, 0)),
            pl.BlockSpec((256, 2 * NS), lambda at: (0, 0)),
        ],
        out_shape=[
            shape((4, COMPS, 2 * NS), BF16),
            shape((6, COMPS, 128), BF16),
            shape((256, 2 * NS), F32),
        ],
        scratch_shapes=[
            pltpu.VMEM((128, NS), BF16),
            pltpu.VMEM((128, 128), BF16),
            pltpu.VMEM((64, 2 * NS), F32),
            pltpu.VMEM((SPAN, NS), F32),
        ],
        compiler_params=big,
        cost_estimate=cost(2e10, 4e7),
        name="model",
    )(sky, everyone, own)
    drive, squares = pl.pallas_call(
        gradient_kernel,
        grid=(STEPS,),
        in_specs=[
            SMEM,
            SMEM,
            pl.BlockSpec((4, SPAN, 2 * NS), lambda at: (0, at, 0)),
            pl.BlockSpec((6, SPAN, 128), lambda at: (0, at, 0)),
        ]
        + [VMEM] * 7,
        out_specs=[VMEM, VMEM],
        out_shape=[shape((64, 128), F32), shape((BLOCKS, 128), F32)],
        scratch_shapes=[
            pltpu.VMEM((256, 2 * NS), BF16),
            pltpu.VMEM((256, 256), BF16),
            pltpu.VMEM((64, 128), F32),
        ],
        compiler_params=big,
        cost_estimate=cost(7e9, 3e7),
        name="gradient",
    )(band, block, far, weighted, vis, flag_mask, incoming, model, own, duals, consensus)
    squares = lax.all_to_all(squares, "stn", 0, 0, tiled=True)
    jones_next, shared = pl.pallas_call(
        update_kernel,
        out_shape=[shape((8, DIRS, OWN), F32), shape((BANDS, 64, 128), F32)],
        in_specs=[VMEM] * 4,
        out_specs=[VMEM, VMEM],
        name="update",
    )(squares, drive, own, duals)
    gathered = lax.all_to_all(shared, "freq", 0, 0, tiled=True)
    duals_next, consensus_next = pl.pallas_call(
        finish_kernel,
        grid=(1,),
        out_shape=[shape((8, DIRS, OWN), F32), shape((4, 8, DIRS, OWN), F32)],
        in_specs=[SMEM, VMEM, pl.BlockSpec((1, 64, 128), lambda at: (0, 0, 0))],
        out_specs=[VMEM, VMEM],
        name="finish",
    )(band, gathered, shared)
    return (jones_next[None], duals_next[None], consensus_next)


def solution(mesh):
    placed = (
        P("freq", None, "stn", None),
        P("stn", None),
        P(None, "stn"),
        P(),
        P(),
        P(),
        P(),
        P(),
        P("freq", None, None, "stn"),
        P("freq", None, None, "stn"),
        P(None, None, None, "stn"),
    )
    return jax.shard_map(
        local,
        mesh=mesh,
        in_specs=placed,
        out_specs=(
            P("freq", None, None, "stn"),
            P("freq", None, None, "stn"),
            P(None, None, None, "stn"),
        ),
        check_vma=False,
    )
```

```python
import math

import jax
import jax.numpy as jnp
import numpy as np
from jax import lax
from jax.experimental import pallas as pl
from jax.experimental.pallas import tpu as pltpu
from jax.sharding import PartitionSpec as P

DIRS = 16
COMPS = 1536
BANDS = 16
BLOCKS = 16
NS = 1024
OWN = 64
ENTRIES = 131072
PENALTY = 40.0
STEP_SIZE = 0.5
F32 = jnp.float32
BF16 = jnp.bfloat16
SPAN = 256
CHUNK = 256
STEPS = COMPS // SPAN
VMEM = pl.BlockSpec(memory_space=pltpu.VMEM)
SMEM = pl.BlockSpec(memory_space=pltpu.SMEM)


def turn_polynomials():
    nodes = (np.cos(np.pi * (np.arange(64) + 0.5) / 64) + 1.0) / 8.0
    root = np.sqrt(nodes)
    scale = np.sqrt(2.0)
    fits = []
    for values in (scale * np.cos(np.pi * root), -scale * np.sin(np.pi * root) / root):
        fit = np.polynomial.Chebyshev.fit(nodes, values, DEGREE, domain=[0, 0.25])
        fits.append([float(v) for v in fit.convert(kind=np.polynomial.Polynomial).coef])
    return fits


DEGREE = 3
COS_POLY, SIN_POLY = turn_polynomials()


def legendre_rows():
    centre = (2.0 * np.arange(BANDS) + 1.0) / BANDS - 1.0
    return np.stack(
        [
            np.ones_like(centre),
            centre,
            0.5 * (3.0 * centre * centre - 1.0),
            0.5 * (5.0 * centre * centre * centre - 3.0 * centre),
        ],
        axis=1,
    )


def horner(coefs, value):
    total = coefs[-1]
    for coef in coefs[-2::-1]:
        total = total * value + coef
    return total


def phases(turns):
    frac = turns - jnp.floor(turns + 0.5)
    square = frac * frac
    half_cos = horner(COS_POLY, square)
    half_sin = frac * horner(SIN_POLY, square)
    real = 1.0 - half_sin * half_sin
    imag = half_sin * half_cos
    return real.astype(BF16).astype(F32), imag.astype(BF16).astype(F32)


def split3(value):
    high = value.astype(BF16).astype(F32)
    rest = value - high
    middle = rest.astype(BF16).astype(F32)
    return high, middle, (rest - middle).astype(BF16).astype(F32)


def band_basis(band):
    centre = (2.0 * band.astype(F32) + 1.0) / BANDS - 1.0
    return (
        jnp.float32(1.0),
        centre,
        0.5 * (3.0 * centre * centre - 1.0),
        0.5 * (5.0 * centre * centre * centre - 3.0 * centre),
    )


def gains_rows(ref, lead=()):
    groups = []
    for column in range(2):
        for part in range(2):
            at = 2 * column + part
            groups.append(jnp.concatenate([ref[lead + (at,)], ref[lead + (4 + at,)]], axis=1))
    return jnp.concatenate(groups, axis=0)


def put_gains(ref, rows, lead=()):
    for column in range(2):
        for part in range(2):
            at = 2 * column + part
            group = rows[at * 16 : at * 16 + 16]
            ref[lead + (at,)] = group[:, :64]
            ref[lead + (4 + at,)] = group[:, 64:]


def packet_kernel(jones_ref, stations_ref, own_ref, copies_ref):
    place = jnp.concatenate([stations_ref[...], stations_ref[...]], axis=1)
    rows = jnp.concatenate([gains_rows(jones_ref), place, jnp.zeros((5, 128), F32)], axis=0)
    own_ref[...] = rows
    copies_ref[...] = jnp.broadcast_to(rows[None], copies_ref.shape)


def prepare_kernel(
    band_ref,
    vis_ref,
    mask_ref,
    dirs_ref,
    flux_ref,
    pol_ref,
    index_ref,
    clusters_ref,
    out_ref,
    sky_ref,
):
    @pl.when(pl.program_id(0) == 0)
    def _():
        prepare_sky(band_ref, dirs_ref, flux_ref, pol_ref, index_ref, clusters_ref, sky_ref)

    mask = mask_ref[...].astype(F32)

    def put(pair, real, imag):
        turned = jnp.concatenate([real, imag], axis=0).T.astype(BF16)
        for dest in range(2):
            out_ref[dest, pair * 64 : pair * 64 + 64, :] = turned[dest * 64 : dest * 64 + 64]

    for pair in range(4):
        put(pair, vis_ref[2 * pair] * mask, vis_ref[2 * pair + 1] * mask)
    lower = lax.broadcasted_iota(jnp.int32, (1, 128), 1) < 64
    turned = jnp.concatenate([mask, mask], axis=0).T
    for dest in range(2):
        at = dest * 64
        packed = jnp.where(lower, turned[at : at + 32], turned[at + 32 : at + 64])
        out_ref[dest, 256:288, :] = packed.astype(BF16)


def flat(ref):
    return jnp.concatenate([ref[at : at + 1, :] for at in range(COMPS // 128)], axis=1)


def prepare_sky(band_ref, dirs_ref, flux_ref, pol_ref, index_ref, clusters_ref, out_ref):
    ratio = 0.5 + 3.0 * (band_ref[0].astype(F32) + 0.5) / BANDS
    dir_l = dirs_ref[0:1, :]
    dir_m = dirs_ref[1:2, :]
    dir_n = jnp.sqrt(1.0 - dir_l * dir_l - dir_m * dir_m) - 1.0
    log_ratio = jnp.log(jnp.full((1, COMPS), ratio, F32))
    factor = jnp.exp(flat(index_ref) * log_ratio)
    flux = flat(flux_ref)
    stokes_q = pol_ref[0:1, :]
    rows = [
        dir_l * ratio,
        dir_m * ratio,
        dir_n * ratio,
        (flux + stokes_q) * factor,
        pol_ref[1:2, :] * factor,
        (flux - stokes_q) * factor,
    ]
    row_at = lax.broadcasted_iota(jnp.int32, (8, COMPS), 0)
    stacked = jnp.zeros((8, COMPS), F32)
    for at, row in enumerate(rows):
        stacked = jnp.where(row_at == at, row, stacked)
    high, middle, low = split3(stacked)
    table = jnp.concatenate(
        [high, high, high, middle, middle, low, jnp.zeros((80, COMPS), F32)], axis=0
    ).astype(BF16)
    clusters = flat(clusters_ref)
    hot = (lax.broadcasted_iota(jnp.int32, (16, COMPS), 0) == clusters).astype(F32)
    before = (
        lax.broadcasted_iota(jnp.int32, (128, 128), 0)
        < lax.broadcasted_iota(jnp.int32, (128, 128), 1)
    ).astype(BF16)
    seen = jnp.zeros((16, 1), F32)
    ranks = []
    for at in range(COMPS // 128):
        part = hot[:, at * 128 : at * 128 + 128]
        inside = jnp.dot(part.astype(BF16), before, preferred_element_type=F32) + seen
        ranks.append(jnp.sum(inside * part, axis=0, keepdims=True))
        seen = seen + jnp.sum(part, axis=1, keepdims=True)
    place = 16 * jnp.concatenate(ranks, axis=1).astype(jnp.int32) + clusters
    for at in range(COMPS // 256):
        target = lax.broadcasted_iota(jnp.int32, (256, COMPS), 0) + at * 256
        chosen = (target == place).astype(F32).astype(BF16)
        out_ref[at * 256 : at * 256 + 256, :] = lax.dot_general(
            chosen, table, (((1,), (1,)), ((), ())), preferred_element_type=F32
        ).astype(BF16)


def station_operand(rows8):
    high, middle, low = split3(rows8)
    width = rows8.shape[1]
    return jnp.concatenate(
        [high, middle, low, high, middle, high, jnp.zeros((80, width), F32)], axis=0
    ).astype(BF16)


def model_kernel(
    sky_ref, all_ref, own_ref, far_ref, weighted_ref, model_ref, geo_ref, geo_own_ref, gains_ref
):
    step = pl.program_id(0)
    lower = lax.broadcasted_iota(jnp.int32, (1, 128), 1) < 64

    @pl.when(step == 0)
    def _():
        model_ref[...] = jnp.zeros_like(model_ref)
        geo_own_ref[...] = station_operand(own_ref[64:72, :])
        for tile in range(8):
            first, second = all_ref[2 * tile], all_ref[2 * tile + 1]
            lanes = slice(tile * 128, tile * 128 + 128)
            geo_ref[:, lanes] = station_operand(jnp.where(lower, first[64:72], second[64:72]))
            low_part = jnp.where(lower, first[0:64], pltpu.roll(second[0:64], 64, 1))
            high_part = jnp.where(lower, pltpu.roll(first[0:64], 64, 1), second[0:64])
            gains_ref[:, lanes] = low_part
            gains_ref[:, 1024 + tile * 128 : 1024 + tile * 128 + 128] = high_part

    sky = sky_ref[...]
    own_re, own_im = phases(jnp.dot(sky, geo_own_ref[...], preferred_element_type=F32))
    source = lax.broadcasted_iota(jnp.int32, (128, 384), 0)
    target = 3 + lax.broadcasted_iota(jnp.int32, (128, 384), 1) // 128
    select = (source == target) | (source == target + 24) | (source == target + 40)
    weights = jnp.dot(sky, select.astype(F32).astype(BF16), preferred_element_type=F32)
    weighted = []
    for flux in range(3):
        weight = weights[:, flux * 128 : flux * 128 + 128]
        pair = ((own_re * weight).astype(BF16), (own_im * weight).astype(BF16))
        weighted_ref[2 * flux] = pair[0]
        weighted_ref[2 * flux + 1] = pair[1]
        weighted.append((pair[0].astype(F32), pair[1].astype(F32)))
    gains = [jnp.concatenate([own_ref[at * 16 : at * 16 + 16]] * (SPAN // 16), axis=0) for at in range(4)]
    near_re, near_im = [], []
    for first, second in ((0, 1), (1, 2)):
        (ar, ai), (br, bi) = weighted[first], weighted[second]
        real = gains[0] * ar - gains[1] * ai + gains[2] * br - gains[3] * bi
        imag = gains[0] * ai + gains[1] * ar + gains[2] * bi + gains[3] * br
        near_re.append(real.T)
        near_im.append(imag.T)
    near = jnp.concatenate(
        [
            jnp.concatenate(near_re + near_im, axis=1),
            jnp.concatenate(near_im + [-near_re[0], -near_re[1]], axis=1),
        ],
        axis=0,
    ).astype(BF16)
    for lane in range(0, NS, CHUNK):
        turns = jnp.dot(
            sky, geo_ref[:, lane : lane + CHUNK], preferred_element_type=F32
        )
        for at in range(0, SPAN, 16):
            rows = slice(at, at + 16)
            real, imag = phases(turns[rows])
            for row in range(2):
                lanes = slice(row * NS + lane, row * NS + lane + CHUNK)
                for column in range(2):
                    gain_re = gains_ref[column * 32 : column * 32 + 16, lanes]
                    gain_im = gains_ref[column * 32 + 16 : column * 32 + 32, lanes]
                    far_ref[column, rows, lanes] = (real * gain_re - imag * gain_im).astype(BF16)
                    far_ref[2 + column, rows, lanes] = (real * gain_im + imag * gain_re).astype(
                        BF16
                    )
        for row in range(2):
            lanes = slice(row * NS + lane, row * NS + lane + CHUNK)
            far = far_ref[:, :, lanes].reshape(4 * SPAN, CHUNK)
            model_ref[:, lanes] += jnp.dot(near, far, preferred_element_type=F32)


def gradient_kernel(
    band_ref,
    block_ref,
    far_ref,
    weighted_ref,
    vis_ref,
    mask_ref,
    got_ref,
    model_ref,
    own_ref,
    duals_ref,
    consensus_ref,
    drive_ref,
    square_ref,
    both_ref,
    near_ref,
    sum_ref,
    turned_ref,
):
    step = pl.program_id(0)
    own_tile = block_ref[0] // 2

    @pl.when(step == 0)
    def _():
        sum_ref[...] = jnp.zeros_like(sum_ref)
        lower = lax.broadcasted_iota(jnp.int32, (1, 128), 1) < 64

        def both_sides(tile, lane):
            lanes = pl.ds(lane, 128)
            far_lanes = pl.ds(NS + lane, 128)
            mask = mask_ref[:, lanes].astype(F32)

            def halves(top, count):
                first = got_ref[2 * tile, top : top + count, :].astype(F32)
                second = got_ref[2 * tile + 1, top : top + count, :].astype(F32)
                return (
                    jnp.where(lower, first, pltpu.roll(second, 64, 1)),
                    jnp.where(lower, pltpu.roll(first, 64, 1), second),
                )

            mask_both = mask + jnp.concatenate(halves(256, 32), axis=0)
            for row in range(2):
                for column in range(2):
                    real, imag = halves((2 * column + row) * 64, 64)
                    for part, other in ((0, real), (1, -imag)):
                        top = part * 128 + row * 64
                        vis = vis_ref[4 * row + 2 * column + part, :, lanes]
                        model = model_ref[top : top + 64, far_lanes if column else lanes]
                        yield top, column, vis * mask + other - mask_both * model

        for tile in range(8):
            for top, column, value in both_sides(tile, tile * 128):
                at = column * NS + tile * 128
                both_ref[top : top + 64, at : at + 128] = value.astype(BF16)
        for top, column, value in both_sides(own_tile, pl.multiple_of(own_tile * 128, 128)):
            near_ref[top : top + 64, column * 128 : column * 128 + 128] = (
                value - value.astype(BF16).astype(F32)
            ).astype(BF16)
        for lane in range(0, 2 * NS, 256):
            turned_ref[lane : lane + 256, :] = both_ref[:, lane : lane + 256].T

    product = jnp.dot(
        far_ref[...].reshape(4 * SPAN, 2 * NS), turned_ref[...], preferred_element_type=F32
    )
    lane = pl.multiple_of(own_tile * 128, 128)
    beside = jnp.concatenate(
        [
            far_ref[:, :, pl.ds(lane, 128)].reshape(4 * SPAN, 128),
            far_ref[:, :, pl.ds(NS + lane, 128)].reshape(4 * SPAN, 128),
        ],
        axis=1,
    )
    product = product + lax.dot_general(
        beside, near_ref[...], (((1,), (1,)), ((), ())), preferred_element_type=F32
    )
    terms = []
    for column in range(2):
        real_rows = product[column * SPAN : column * SPAN + SPAN]
        imag_rows = product[(2 + column) * SPAN : (2 + column) * SPAN + SPAN]
        terms.append(
            (
                real_rows[:, :128] - imag_rows[:, 128:],
                imag_rows[:, :128] + real_rows[:, 128:],
            )
        )
    weighted = [weighted_ref[at].astype(F32) for at in range(6)]
    for column, (first, second) in enumerate(((0, 1), (1, 2))):
        real = jnp.zeros((SPAN, 128), F32)
        imag = jnp.zeros((SPAN, 128), F32)
        for (tr, ti), flux in zip(terms, (first, second)):
            wr, wi = weighted[2 * flux], weighted[2 * flux + 1]
            real = real + (tr * wr + ti * wi)
            imag = imag + (ti * wr - tr * wi)
        for part, value in enumerate((real, imag)):
            at = (2 * column + part) * 16
            sum_ref[at : at + 16] += jnp.sum(value.reshape(SPAN // 16, 16, 128), axis=0)

    @pl.when(step == STEPS - 1)
    def _():
        basis = band_basis(band_ref[0])
        poly = jnp.zeros((64, 128), F32)
        for at in range(4):
            poly = poly + basis[at] * gains_rows(consensus_ref, (at,))
        penalty = PENALTY / 2.0 * (own_ref[0:64, :] - poly + gains_rows(duals_ref))
        drive = penalty - sum_ref[...]
        drive_ref[...] = drive
        square_ref[...] = jnp.broadcast_to(
            jnp.sum(drive * drive, axis=0, keepdims=True), square_ref.shape
        )


def update_kernel(squares_ref, drive_ref, own_ref, duals_ref, next_ref, shared_ref):
    total = jnp.sum(squares_ref[...], axis=(0, 1), keepdims=True)
    length = STEP_SIZE / jnp.sqrt(total / ENTRIES + 1e-6)
    rows = own_ref[0:64, :] - length * drive_ref[...]
    put_gains(next_ref, rows)
    shared_ref[...] = jnp.broadcast_to((rows + gains_rows(duals_ref))[None], shared_ref.shape)


def finish_kernel(band_ref, shared_ref, own_ref, duals_ref, consensus_ref):
    table = legendre_rows()
    gram = table.T @ table
    lower = np.linalg.cholesky(gram)
    sums = []
    for at in range(4):
        total = shared_ref[0] * float(table[0, at])
        for band in range(1, BANDS):
            total = total + shared_ref[band] * float(table[band, at])
        sums.append(total)
    forward = []
    for row in range(4):
        current = sums[row]
        for col in range(row):
            current = current - float(lower[row, col]) * forward[col]
        forward.append(current * float(1.0 / lower[row, row]))
    backward = [None] * 4
    for row in (3, 2, 1, 0):
        current = forward[row]
        for col in range(row + 1, 4):
            current = current - float(lower[col, row]) * backward[col]
        backward[row] = current * float(1.0 / lower[row, row])
    basis = band_basis(band_ref[0])
    poly = jnp.zeros((64, 128), F32)
    for at in range(4):
        put_gains(consensus_ref, backward[at], (at,))
        poly = poly + basis[at] * backward[at]
    put_gains(duals_ref, own_ref[0] - poly)


def cost(flops, moved):
    return pl.CostEstimate(flops=int(flops), bytes_accessed=int(moved), transcendentals=0)


BIG = pltpu.CompilerParams(vmem_limit_bytes=56 * 1024 * 1024)
shape = jax.ShapeDtypeStruct


def call_model(sky, everyone, own):
    return pl.pallas_call(
        model_kernel,
        grid=(STEPS,),
        in_specs=[
            pl.BlockSpec((SPAN, 128), lambda at: (at, 0)),
            VMEM,
            VMEM,
        ],
        out_specs=[
            pl.BlockSpec((4, SPAN, 2 * NS), lambda at: (0, at, 0)),
            pl.BlockSpec((6, SPAN, 128), lambda at: (0, at, 0)),
            pl.BlockSpec((256, 2 * NS), lambda at: (0, 0)),
        ],
        out_shape=[
            shape((4, COMPS, 2 * NS), BF16),
            shape((6, COMPS, 128), BF16),
            shape((256, 2 * NS), F32),
        ],
        scratch_shapes=[
            pltpu.VMEM((128, NS), BF16),
            pltpu.VMEM((128, 128), BF16),
            pltpu.VMEM((64, 2 * NS), F32),
        ],
        compiler_params=BIG,
        cost_estimate=cost(2e10, 4e7),
        name="model",
    )(sky, everyone, own)


def call_gradient(*operands):
    return pl.pallas_call(
        gradient_kernel,
        grid=(STEPS,),
        in_specs=[
            SMEM,
            SMEM,
            pl.BlockSpec((4, SPAN, 2 * NS), lambda at: (0, at, 0)),
            pl.BlockSpec((6, SPAN, 128), lambda at: (0, at, 0)),
        ]
        + [VMEM] * 7,
        out_specs=[VMEM, VMEM],
        out_shape=[shape((64, 128), F32), shape((BLOCKS, 128), F32)],
        scratch_shapes=[
            pltpu.VMEM((256, 2 * NS), BF16),
            pltpu.VMEM((256, 256), BF16),
            pltpu.VMEM((64, 128), F32),
            pltpu.VMEM((2 * NS, 256), BF16),
        ],
        compiler_params=BIG,
        cost_estimate=cost(7e9, 3e7),
        name="gradient",
    )(*operands)


def local(
    visibilities,
    flag_mask,
    stations,
    directions,
    intensity,
    polarized,
    spectral,
    clusters,
    jones_gains,
    scaled_duals,
    consensus,
):
    band = lax.axis_index("freq").reshape(1).astype(jnp.int32)
    block = lax.axis_index("stn").reshape(1).astype(jnp.int32)
    vis, jones, duals = visibilities[0], jones_gains[0], scaled_duals[0]
    own, copies = pl.pallas_call(
        packet_kernel,
        out_shape=[shape((72, 128), F32), shape((BLOCKS, 72, 128), F32)],
        in_specs=[VMEM] * 2,
        out_specs=[VMEM, VMEM],
        name="packet",
    )(jones, stations)
    everyone = lax.all_to_all(copies, "stn", 0, 0, tiled=True)
    outgoing, sky = pl.pallas_call(
        prepare_kernel,
        grid=(8,),
        in_specs=[
            SMEM,
            pl.BlockSpec((8, OWN, 128), lambda at: (0, 0, at)),
            pl.BlockSpec((OWN, 128), lambda at: (0, at)),
        ]
        + [VMEM] * 5,
        out_specs=[pl.BlockSpec((2, 288, 128), lambda at: (at, 0, 0)), VMEM],
        out_shape=[shape((BLOCKS, 288, 128), BF16), shape((COMPS, 128), BF16)],
        compiler_params=BIG,
        cost_estimate=cost(4e9, 1e6),
        name="prepare",
    )(
        band,
        vis,
        flag_mask,
        directions,
        intensity.reshape(COMPS // 128, 128),
        polarized,
        spectral.reshape(COMPS // 128, 128),
        clusters.reshape(COMPS // 128, 128),
    )
    incoming = lax.all_to_all(outgoing, "stn", 0, 0, tiled=True)
    far, weighted, model = call_model(sky, everyone, own)
    drive, squares = call_gradient(
        band, block, far, weighted, vis, flag_mask, incoming, model, own, duals, consensus
    )
    squares = lax.all_to_all(squares, "stn", 0, 0, tiled=True)
    jones_next, shared = pl.pallas_call(
        update_kernel,
        out_shape=[shape((8, DIRS, OWN), F32), shape((BANDS, 64, 128), F32)],
        in_specs=[VMEM] * 4,
        out_specs=[VMEM, VMEM],
        name="update",
    )(squares, drive, own, duals)
    gathered = lax.all_to_all(shared, "freq", 0, 0, tiled=True)
    duals_next, consensus_next = pl.pallas_call(
        finish_kernel,
        grid=(1,),
        out_shape=[shape((8, DIRS, OWN), F32), shape((4, 8, DIRS, OWN), F32)],
        in_specs=[SMEM, VMEM, pl.BlockSpec((1, 64, 128), lambda at: (0, 0, 0))],
        out_specs=[VMEM, VMEM],
        name="finish",
    )(band, gathered, shared)
    return (jones_next[None], duals_next[None], consensus_next)


def solution(mesh):
    placed = (
        P("freq", None, "stn", None),
        P("stn", None),
        P(None, "stn"),
        P(),
        P(),
        P(),
        P(),
        P(),
        P("freq", None, None, "stn"),
        P("freq", None, None, "stn"),
        P(None, None, None, "stn"),
    )
    return jax.shard_map(
        local,
        mesh=mesh,
        in_specs=placed,
        out_specs=(
            P("freq", None, None, "stn"),
            P("freq", None, None, "stn"),
            P(None, None, None, "stn"),
        ),
        check_vma=False,
    )
```

```python
import math

import jax
import jax.numpy as jnp
import numpy as np
from jax import lax
from jax.experimental import pallas as pl
from jax.experimental.pallas import tpu as pltpu
from jax.sharding import PartitionSpec as P

DIRS = 16
COMPS = 1536
BANDS = 16
BLOCKS = 16
NS = 1024
OWN = 64
ENTRIES = 131072
PENALTY = 40.0
STEP_SIZE = 0.5
F32 = jnp.float32
BF16 = jnp.bfloat16
SPAN = 384
CHUNK = 256
STEPS = COMPS // SPAN
VMEM = pl.BlockSpec(memory_space=pltpu.VMEM)
SMEM = pl.BlockSpec(memory_space=pltpu.SMEM)


def turn_polynomials():
    nodes = (np.cos(np.pi * (np.arange(64) + 0.5) / 64) + 1.0) / 8.0
    root = np.sqrt(nodes)
    scale = np.sqrt(2.0)
    fits = []
    for values in (scale * np.cos(np.pi * root), -scale * np.sin(np.pi * root) / root):
        fit = np.polynomial.Chebyshev.fit(nodes, values, DEGREE, domain=[0, 0.25])
        fits.append([float(v) for v in fit.convert(kind=np.polynomial.Polynomial).coef])
    return fits


DEGREE = 3
COS_POLY, SIN_POLY = turn_polynomials()


def legendre_rows():
    centre = (2.0 * np.arange(BANDS) + 1.0) / BANDS - 1.0
    return np.stack(
        [
            np.ones_like(centre),
            centre,
            0.5 * (3.0 * centre * centre - 1.0),
            0.5 * (5.0 * centre * centre * centre - 3.0 * centre),
        ],
        axis=1,
    )


def horner(coefs, value):
    total = coefs[-1]
    for coef in coefs[-2::-1]:
        total = total * value + coef
    return total


def phases(turns):
    frac = turns - jnp.floor(turns + 0.5)
    square = frac * frac
    half_cos = horner(COS_POLY, square)
    half_sin = frac * horner(SIN_POLY, square)
    real = 1.0 - half_sin * half_sin
    imag = half_sin * half_cos
    return real.astype(BF16).astype(F32), imag.astype(BF16).astype(F32)


def split3(value):
    high = value.astype(BF16).astype(F32)
    rest = value - high
    middle = rest.astype(BF16).astype(F32)
    return high, middle, (rest - middle).astype(BF16).astype(F32)


def band_basis(band):
    centre = (2.0 * band.astype(F32) + 1.0) / BANDS - 1.0
    return (
        jnp.float32(1.0),
        centre,
        0.5 * (3.0 * centre * centre - 1.0),
        0.5 * (5.0 * centre * centre * centre - 3.0 * centre),
    )


def gains_rows(ref, lead=()):
    groups = []
    for column in range(2):
        for part in range(2):
            at = 2 * column + part
            groups.append(jnp.concatenate([ref[lead + (at,)], ref[lead + (4 + at,)]], axis=1))
    return jnp.concatenate(groups, axis=0)


def put_gains(ref, rows, lead=()):
    for column in range(2):
        for part in range(2):
            at = 2 * column + part
            group = rows[at * 16 : at * 16 + 16]
            ref[lead + (at,)] = group[:, :64]
            ref[lead + (4 + at,)] = group[:, 64:]


def packet_kernel(jones_ref, stations_ref, own_ref, copies_ref):
    place = jnp.concatenate([stations_ref[...], stations_ref[...]], axis=1)
    rows = jnp.concatenate([gains_rows(jones_ref), place, jnp.zeros((5, 128), F32)], axis=0)
    own_ref[...] = rows
    copies_ref[...] = jnp.broadcast_to(rows[None], copies_ref.shape)


def prepare_kernel(
    band_ref,
    vis_ref,
    mask_ref,
    dirs_ref,
    flux_ref,
    pol_ref,
    index_ref,
    clusters_ref,
    out_ref,
    sky_ref,
):
    @pl.when(pl.program_id(0) == 0)
    def _():
        prepare_sky(band_ref, dirs_ref, flux_ref, pol_ref, index_ref, clusters_ref, sky_ref)

    mask = mask_ref[...].astype(F32)

    def put(pair, real, imag):
        turned = jnp.concatenate([real, imag], axis=0).T.astype(BF16)
        for dest in range(2):
            out_ref[dest, pair * 64 : pair * 64 + 64, :] = turned[dest * 64 : dest * 64 + 64]

    for pair in range(4):
        put(pair, vis_ref[2 * pair] * mask, vis_ref[2 * pair + 1] * mask)
    lower = lax.broadcasted_iota(jnp.int32, (1, 128), 1) < 64
    turned = jnp.concatenate([mask, mask], axis=0).T
    for dest in range(2):
        at = dest * 64
        packed = jnp.where(lower, turned[at : at + 32], turned[at + 32 : at + 64])
        out_ref[dest, 256:288, :] = packed.astype(BF16)


def flat(ref):
    return jnp.concatenate([ref[at : at + 1, :] for at in range(COMPS // 128)], axis=1)


def prepare_sky(band_ref, dirs_ref, flux_ref, pol_ref, index_ref, clusters_ref, out_ref):
    ratio = 0.5 + 3.0 * (band_ref[0].astype(F32) + 0.5) / BANDS
    dir_l = dirs_ref[0:1, :]
    dir_m = dirs_ref[1:2, :]
    dir_n = jnp.sqrt(1.0 - dir_l * dir_l - dir_m * dir_m) - 1.0
    log_ratio = jnp.log(jnp.full((1, COMPS), ratio, F32))
    factor = jnp.exp(flat(index_ref) * log_ratio)
    flux = flat(flux_ref)
    stokes_q = pol_ref[0:1, :]
    rows = [
        dir_l * ratio,
        dir_m * ratio,
        dir_n * ratio,
        (flux + stokes_q) * factor,
        pol_ref[1:2, :] * factor,
        (flux - stokes_q) * factor,
    ]
    row_at = lax.broadcasted_iota(jnp.int32, (8, COMPS), 0)
    stacked = jnp.zeros((8, COMPS), F32)
    for at, row in enumerate(rows):
        stacked = jnp.where(row_at == at, row, stacked)
    high, middle, low = split3(stacked)
    table = jnp.concatenate(
        [high, high, high, middle, middle, low, jnp.zeros((80, COMPS), F32)], axis=0
    ).astype(BF16)
    clusters = flat(clusters_ref)
    hot = (lax.broadcasted_iota(jnp.int32, (16, COMPS), 0) == clusters).astype(F32)
    before = (
        lax.broadcasted_iota(jnp.int32, (128, 128), 0)
        < lax.broadcasted_iota(jnp.int32, (128, 128), 1)
    ).astype(BF16)
    seen = jnp.zeros((16, 1), F32)
    ranks = []
    for at in range(COMPS // 128):
        part = hot[:, at * 128 : at * 128 + 128]
        inside = jnp.dot(part.astype(BF16), before, preferred_element_type=F32) + seen
        ranks.append(jnp.sum(inside * part, axis=0, keepdims=True))
        seen = seen + jnp.sum(part, axis=1, keepdims=True)
    place = 16 * jnp.concatenate(ranks, axis=1).astype(jnp.int32) + clusters
    for at in range(COMPS // 256):
        target = lax.broadcasted_iota(jnp.int32, (256, COMPS), 0) + at * 256
        chosen = (target == place).astype(F32).astype(BF16)
        out_ref[at * 256 : at * 256 + 256, :] = lax.dot_general(
            chosen, table, (((1,), (1,)), ((), ())), preferred_element_type=F32
        ).astype(BF16)


def station_operand(rows8):
    high, middle, low = split3(rows8)
    width = rows8.shape[1]
    return jnp.concatenate(
        [high, middle, low, high, middle, high, jnp.zeros((80, width), F32)], axis=0
    ).astype(BF16)


def model_kernel(
    sky_ref, all_ref, own_ref, far_ref, weighted_ref, model_ref, geo_ref, geo_own_ref, gains_ref
):
    step = pl.program_id(0)
    lower = lax.broadcasted_iota(jnp.int32, (1, 128), 1) < 64

    @pl.when(step == 0)
    def _():
        model_ref[...] = jnp.zeros_like(model_ref)
        geo_own_ref[...] = station_operand(own_ref[64:72, :])
        for tile in range(8):
            first, second = all_ref[2 * tile], all_ref[2 * tile + 1]
            lanes = slice(tile * 128, tile * 128 + 128)
            geo_ref[:, lanes] = station_operand(jnp.where(lower, first[64:72], second[64:72]))
            low_part = jnp.where(lower, first[0:64], pltpu.roll(second[0:64], 64, 1))
            high_part = jnp.where(lower, pltpu.roll(first[0:64], 64, 1), second[0:64])
            gains_ref[:, lanes] = low_part
            gains_ref[:, 1024 + tile * 128 : 1024 + tile * 128 + 128] = high_part

    sky = sky_ref[...]
    own_re, own_im = phases(jnp.dot(sky, geo_own_ref[...], preferred_element_type=F32))
    source = lax.broadcasted_iota(jnp.int32, (128, 384), 0)
    target = 3 + lax.broadcasted_iota(jnp.int32, (128, 384), 1) // 128
    select = (source == target) | (source == target + 24) | (source == target + 40)
    weights = jnp.dot(sky, select.astype(F32).astype(BF16), preferred_element_type=F32)
    weighted = []
    for flux in range(3):
        weight = weights[:, flux * 128 : flux * 128 + 128]
        pair = ((own_re * weight).astype(BF16), (own_im * weight).astype(BF16))
        weighted_ref[2 * flux] = pair[0]
        weighted_ref[2 * flux + 1] = pair[1]
        weighted.append((pair[0].astype(F32), pair[1].astype(F32)))
    gains = [jnp.concatenate([own_ref[at * 16 : at * 16 + 16]] * (SPAN // 16), axis=0) for at in range(4)]
    near_re, near_im = [], []
    for first, second in ((0, 1), (1, 2)):
        (ar, ai), (br, bi) = weighted[first], weighted[second]
        real = gains[0] * ar - gains[1] * ai + gains[2] * br - gains[3] * bi
        imag = gains[0] * ai + gains[1] * ar + gains[2] * bi + gains[3] * br
        near_re.append(real.T)
        near_im.append(imag.T)
    near = jnp.concatenate(
        [
            jnp.concatenate(near_re + near_im, axis=1),
            jnp.concatenate(near_im + [-near_re[0], -near_re[1]], axis=1),
        ],
        axis=0,
    ).astype(BF16)
    for lane in range(0, NS, CHUNK):
        turns = jnp.dot(
            sky, geo_ref[:, lane : lane + CHUNK], preferred_element_type=F32
        )
        for at in range(0, SPAN, 16):
            rows = slice(at, at + 16)
            real, imag = phases(turns[rows])
            for row in range(2):
                lanes = slice(row * NS + lane, row * NS + lane + CHUNK)
                for column in range(2):
                    gain_re = gains_ref[column * 32 : column * 32 + 16, lanes]
                    gain_im = gains_ref[column * 32 + 16 : column * 32 + 32, lanes]
                    far_ref[column, rows, lanes] = (real * gain_re - imag * gain_im).astype(BF16)
                    far_ref[2 + column, rows, lanes] = (real * gain_im + imag * gain_re).astype(
                        BF16
                    )
        for row in range(2):
            lanes = slice(row * NS + lane, row * NS + lane + CHUNK)
            far = far_ref[:, :, lanes].reshape(4 * SPAN, CHUNK)
            model_ref[:, lanes] += jnp.dot(near, far, preferred_element_type=F32)


def gradient_kernel(
    band_ref,
    block_ref,
    far_ref,
    weighted_ref,
    vis_ref,
    mask_ref,
    got_ref,
    model_ref,
    own_ref,
    duals_ref,
    consensus_ref,
    drive_ref,
    square_ref,
    both_ref,
    near_ref,
    sum_ref,
    turned_ref,
):
    step = pl.program_id(0)
    own_tile = block_ref[0] // 2

    @pl.when(step == 0)
    def _():
        sum_ref[...] = jnp.zeros_like(sum_ref)
        lower = lax.broadcasted_iota(jnp.int32, (1, 128), 1) < 64

        def both_sides(tile, lane):
            lanes = pl.ds(lane, 128)
            far_lanes = pl.ds(NS + lane, 128)
            mask = mask_ref[:, lanes].astype(F32)

            def halves(top, count):
                first = got_ref[2 * tile, top : top + count, :].astype(F32)
                second = got_ref[2 * tile + 1, top : top + count, :].astype(F32)
                return (
                    jnp.where(lower, first, pltpu.roll(second, 64, 1)),
                    jnp.where(lower, pltpu.roll(first, 64, 1), second),
                )

            mask_both = mask + jnp.concatenate(halves(256, 32), axis=0)
            for row in range(2):
                for column in range(2):
                    real, imag = halves((2 * column + row) * 64, 64)
                    for part, other in ((0, real), (1, -imag)):
                        top = part * 128 + row * 64
                        vis = vis_ref[4 * row + 2 * column + part, :, lanes]
                        model = model_ref[top : top + 64, far_lanes if column else lanes]
                        yield top, column, vis * mask + other - mask_both * model

        for tile in range(8):
            for top, column, value in both_sides(tile, tile * 128):
                at = column * NS + tile * 128
                both_ref[top : top + 64, at : at + 128] = value.astype(BF16)
        for top, column, value in both_sides(own_tile, pl.multiple_of(own_tile * 128, 128)):
            near_ref[top : top + 64, column * 128 : column * 128 + 128] = (
                value - value.astype(BF16).astype(F32)
            ).astype(BF16)
        for lane in range(0, 2 * NS, 256):
            turned_ref[lane : lane + 256, :] = both_ref[:, lane : lane + 256].T

    product = jnp.dot(
        far_ref[...].reshape(4 * SPAN, 2 * NS), turned_ref[...], preferred_element_type=F32
    )
    lane = pl.multiple_of(own_tile * 128, 128)
    beside = jnp.concatenate(
        [
            far_ref[:, :, pl.ds(lane, 128)].reshape(4 * SPAN, 128),
            far_ref[:, :, pl.ds(NS + lane, 128)].reshape(4 * SPAN, 128),
        ],
        axis=1,
    )
    product = product + lax.dot_general(
        beside, near_ref[...], (((1,), (1,)), ((), ())), preferred_element_type=F32
    )
    terms = []
    for column in range(2):
        real_rows = product[column * SPAN : column * SPAN + SPAN]
        imag_rows = product[(2 + column) * SPAN : (2 + column) * SPAN + SPAN]
        terms.append(
            (
                real_rows[:, :128] - imag_rows[:, 128:],
                imag_rows[:, :128] + real_rows[:, 128:],
            )
        )
    weighted = [weighted_ref[at].astype(F32) for at in range(6)]
    for column, (first, second) in enumerate(((0, 1), (1, 2))):
        real = jnp.zeros((SPAN, 128), F32)
        imag = jnp.zeros((SPAN, 128), F32)
        for (tr, ti), flux in zip(terms, (first, second)):
            wr, wi = weighted[2 * flux], weighted[2 * flux + 1]
            real = real + (tr * wr + ti * wi)
            imag = imag + (ti * wr - tr * wi)
        for part, value in enumerate((real, imag)):
            at = (2 * column + part) * 16
            sum_ref[at : at + 16] += jnp.sum(value.reshape(SPAN // 16, 16, 128), axis=0)

    @pl.when(step == STEPS - 1)
    def _():
        basis = band_basis(band_ref[0])
        poly = jnp.zeros((64, 128), F32)
        for at in range(4):
            poly = poly + basis[at] * gains_rows(consensus_ref, (at,))
        penalty = PENALTY / 2.0 * (own_ref[0:64, :] - poly + gains_rows(duals_ref))
        drive = penalty - sum_ref[...]
        drive_ref[...] = drive
        square_ref[...] = jnp.broadcast_to(
            jnp.sum(drive * drive, axis=0, keepdims=True), square_ref.shape
        )


def update_kernel(squares_ref, drive_ref, own_ref, duals_ref, next_ref, shared_ref):
    total = jnp.sum(squares_ref[...], axis=(0, 1), keepdims=True)
    length = STEP_SIZE / jnp.sqrt(total / ENTRIES + 1e-6)
    rows = own_ref[0:64, :] - length * drive_ref[...]
    put_gains(next_ref, rows)
    shared_ref[...] = jnp.broadcast_to((rows + gains_rows(duals_ref))[None], shared_ref.shape)


def finish_kernel(band_ref, shared_ref, own_ref, duals_ref, consensus_ref):
    table = legendre_rows()
    gram = table.T @ table
    lower = np.linalg.cholesky(gram)
    sums = []
    for at in range(4):
        total = shared_ref[0] * float(table[0, at])
        for band in range(1, BANDS):
            total = total + shared_ref[band] * float(table[band, at])
        sums.append(total)
    forward = []
    for row in range(4):
        current = sums[row]
        for col in range(row):
            current = current - float(lower[row, col]) * forward[col]
        forward.append(current * float(1.0 / lower[row, row]))
    backward = [None] * 4
    for row in (3, 2, 1, 0):
        current = forward[row]
        for col in range(row + 1, 4):
            current = current - float(lower[col, row]) * backward[col]
        backward[row] = current * float(1.0 / lower[row, row])
    basis = band_basis(band_ref[0])
    poly = jnp.zeros((64, 128), F32)
    for at in range(4):
        put_gains(consensus_ref, backward[at], (at,))
        poly = poly + basis[at] * backward[at]
    put_gains(duals_ref, own_ref[0] - poly)


def cost(flops, moved):
    return pl.CostEstimate(flops=int(flops), bytes_accessed=int(moved), transcendentals=0)


BIG = pltpu.CompilerParams(vmem_limit_bytes=54 * 1024 * 1024)
shape = jax.ShapeDtypeStruct


def call_model(sky, everyone, own):
    return pl.pallas_call(
        model_kernel,
        grid=(STEPS,),
        in_specs=[
            pl.BlockSpec((SPAN, 128), lambda at: (at, 0)),
            VMEM,
            VMEM,
        ],
        out_specs=[
            pl.BlockSpec((4, SPAN, 2 * NS), lambda at: (0, at, 0)),
            pl.BlockSpec((6, SPAN, 128), lambda at: (0, at, 0)),
            pl.BlockSpec((256, 2 * NS), lambda at: (0, 0)),
        ],
        out_shape=[
            shape((4, COMPS, 2 * NS), BF16),
            shape((6, COMPS, 128), BF16),
            shape((256, 2 * NS), F32),
        ],
        scratch_shapes=[
            pltpu.VMEM((128, NS), BF16),
            pltpu.VMEM((128, 128), BF16),
            pltpu.VMEM((64, 2 * NS), F32),
        ],
        compiler_params=BIG,
        cost_estimate=cost(2e10, 4e7),
        name="model",
    )(sky, everyone, own)


def call_gradient(*operands):
    return pl.pallas_call(
        gradient_kernel,
        grid=(STEPS,),
        in_specs=[
            SMEM,
            SMEM,
            pl.BlockSpec((4, SPAN, 2 * NS), lambda at: (0, at, 0)),
            pl.BlockSpec((6, SPAN, 128), lambda at: (0, at, 0)),
        ]
        + [VMEM] * 7,
        out_specs=[VMEM, VMEM],
        out_shape=[shape((64, 128), F32), shape((BLOCKS, 128), F32)],
        scratch_shapes=[
            pltpu.VMEM((256, 2 * NS), BF16),
            pltpu.VMEM((256, 256), BF16),
            pltpu.VMEM((64, 128), F32),
            pltpu.VMEM((2 * NS, 256), BF16),
        ],
        compiler_params=BIG,
        cost_estimate=cost(7e9, 3e7),
        name="gradient",
    )(*operands)


def local(
    visibilities,
    flag_mask,
    stations,
    directions,
    intensity,
    polarized,
    spectral,
    clusters,
    jones_gains,
    scaled_duals,
    consensus,
):
    band = lax.axis_index("freq").reshape(1).astype(jnp.int32)
    block = lax.axis_index("stn").reshape(1).astype(jnp.int32)
    vis, jones, duals = visibilities[0], jones_gains[0], scaled_duals[0]
    own, copies = pl.pallas_call(
        packet_kernel,
        out_shape=[shape((72, 128), F32), shape((BLOCKS, 72, 128), F32)],
        in_specs=[VMEM] * 2,
        out_specs=[VMEM, VMEM],
        name="packet",
    )(jones, stations)
    everyone = lax.all_to_all(copies, "stn", 0, 0, tiled=True)
    outgoing, sky = pl.pallas_call(
        prepare_kernel,
        grid=(8,),
        in_specs=[
            SMEM,
            pl.BlockSpec((8, OWN, 128), lambda at: (0, 0, at)),
            pl.BlockSpec((OWN, 128), lambda at: (0, at)),
        ]
        + [VMEM] * 5,
        out_specs=[pl.BlockSpec((2, 288, 128), lambda at: (at, 0, 0)), VMEM],
        out_shape=[shape((BLOCKS, 288, 128), BF16), shape((COMPS, 128), BF16)],
        compiler_params=BIG,
        cost_estimate=cost(4e9, 1e6),
        name="prepare",
    )(
        band,
        vis,
        flag_mask,
        directions,
        intensity.reshape(COMPS // 128, 128),
        polarized,
        spectral.reshape(COMPS // 128, 128),
        clusters.reshape(COMPS // 128, 128),
    )
    incoming = lax.all_to_all(outgoing, "stn", 0, 0, tiled=True)
    incoming = pltpu.with_memory_space_constraint(incoming, pltpu.VMEM)
    far, weighted, model = call_model(sky, everyone, own)
    drive, squares = call_gradient(
        band, block, far, weighted, pltpu.with_memory_space_constraint(vis, pltpu.VMEM), flag_mask, incoming, model, own, duals, consensus
    )
    squares = lax.all_to_all(squares, "stn", 0, 0, tiled=True)
    jones_next, shared = pl.pallas_call(
        update_kernel,
        out_shape=[shape((8, DIRS, OWN), F32), shape((BANDS, 64, 128), F32)],
        in_specs=[VMEM] * 4,
        out_specs=[VMEM, VMEM],
        name="update",
    )(squares, drive, own, duals)
    gathered = lax.all_to_all(shared, "freq", 0, 0, tiled=True)
    duals_next, consensus_next = pl.pallas_call(
        finish_kernel,
        grid=(1,),
        out_shape=[shape((8, DIRS, OWN), F32), shape((4, 8, DIRS, OWN), F32)],
        in_specs=[SMEM, VMEM, pl.BlockSpec((1, 64, 128), lambda at: (0, 0, 0))],
        out_specs=[VMEM, VMEM],
        name="finish",
    )(band, gathered, shared)
    return (jones_next[None], duals_next[None], consensus_next)


def solution(mesh):
    placed = (
        P("freq", None, "stn", None),
        P("stn", None),
        P(None, "stn"),
        P(),
        P(),
        P(),
        P(),
        P(),
        P("freq", None, None, "stn"),
        P("freq", None, None, "stn"),
        P(None, None, None, "stn"),
    )
    return jax.shard_map(
        local,
        mesh=mesh,
        in_specs=placed,
        out_specs=(
            P("freq", None, None, "stn"),
            P("freq", None, None, "stn"),
            P(None, None, None, "stn"),
        ),
        check_vma=False,
    )
```

```python
import math

import jax
import jax.numpy as jnp
import numpy as np
from jax import lax
from jax.experimental import pallas as pl
from jax.experimental.pallas import tpu as pltpu
from jax.sharding import PartitionSpec as P

DIRS = 16
COMPS = 1536
BANDS = 16
BLOCKS = 16
NS = 1024
OWN = 64
ENTRIES = 131072
PENALTY = 40.0
STEP_SIZE = 0.5
F32 = jnp.float32
BF16 = jnp.bfloat16
SPAN = 384
CHUNK = 256
STEPS = COMPS // SPAN
VMEM = pl.BlockSpec(memory_space=pltpu.VMEM)
SMEM = pl.BlockSpec(memory_space=pltpu.SMEM)


def turn_polynomials():
    nodes = (np.cos(np.pi * (np.arange(64) + 0.5) / 64) + 1.0) / 8.0
    root = np.sqrt(nodes)
    scale = np.sqrt(2.0)
    fits = []
    for values in (scale * np.cos(np.pi * root), -scale * np.sin(np.pi * root) / root):
        fit = np.polynomial.Chebyshev.fit(nodes, values, DEGREE, domain=[0, 0.25])
        fits.append([float(v) for v in fit.convert(kind=np.polynomial.Polynomial).coef])
    return fits


DEGREE = 3
COS_POLY, SIN_POLY = turn_polynomials()


def legendre_rows():
    centre = (2.0 * np.arange(BANDS) + 1.0) / BANDS - 1.0
    return np.stack(
        [
            np.ones_like(centre),
            centre,
            0.5 * (3.0 * centre * centre - 1.0),
            0.5 * (5.0 * centre * centre * centre - 3.0 * centre),
        ],
        axis=1,
    )


def horner(coefs, value):
    total = coefs[-1]
    for coef in coefs[-2::-1]:
        total = total * value + coef
    return total


def phases(turns):
    frac = turns - jnp.floor(turns + 0.5)
    square = frac * frac
    half_cos = horner(COS_POLY, square)
    half_sin = frac * horner(SIN_POLY, square)
    real = 1.0 - half_sin * half_sin
    imag = half_sin * half_cos
    return real.astype(BF16).astype(F32), imag.astype(BF16).astype(F32)


def split3(value):
    high = value.astype(BF16).astype(F32)
    rest = value - high
    middle = rest.astype(BF16).astype(F32)
    return high, middle, (rest - middle).astype(BF16).astype(F32)


def band_basis(band):
    centre = (2.0 * band.astype(F32) + 1.0) / BANDS - 1.0
    return (
        jnp.float32(1.0),
        centre,
        0.5 * (3.0 * centre * centre - 1.0),
        0.5 * (5.0 * centre * centre * centre - 3.0 * centre),
    )


def gains_rows(ref, lead=()):
    groups = []
    for column in range(2):
        for part in range(2):
            at = 2 * column + part
            groups.append(jnp.concatenate([ref[lead + (at,)], ref[lead + (4 + at,)]], axis=1))
    return jnp.concatenate(groups, axis=0)


def put_gains(ref, rows, lead=()):
    for column in range(2):
        for part in range(2):
            at = 2 * column + part
            group = rows[at * 16 : at * 16 + 16]
            ref[lead + (at,)] = group[:, :64]
            ref[lead + (4 + at,)] = group[:, 64:]


def packet_kernel(jones_ref, stations_ref, own_ref, copies_ref):
    place = jnp.concatenate([stations_ref[...], stations_ref[...]], axis=1)
    rows = jnp.concatenate([gains_rows(jones_ref), place, jnp.zeros((5, 128), F32)], axis=0)
    own_ref[...] = rows
    copies_ref[...] = jnp.broadcast_to(rows[None], copies_ref.shape)


def prepare_kernel(
    band_ref,
    vis_ref,
    mask_ref,
    dirs_ref,
    flux_ref,
    pol_ref,
    index_ref,
    clusters_ref,
    out_ref,
    sky_ref,
):
    @pl.when(pl.program_id(0) == 0)
    def _():
        prepare_sky(band_ref, dirs_ref, flux_ref, pol_ref, index_ref, clusters_ref, sky_ref)

    mask = mask_ref[...].astype(F32)

    def put(pair, real, imag):
        turned = jnp.concatenate([real, imag], axis=0).T.astype(BF16)
        for dest in range(2):
            out_ref[dest, pair * 64 : pair * 64 + 64, :] = turned[dest * 64 : dest * 64 + 64]

    for pair in range(4):
        put(pair, vis_ref[2 * pair] * mask, vis_ref[2 * pair + 1] * mask)
    lower = lax.broadcasted_iota(jnp.int32, (1, 128), 1) < 64
    turned = jnp.concatenate([mask, mask], axis=0).T
    for dest in range(2):
        at = dest * 64
        packed = jnp.where(lower, turned[at : at + 32], turned[at + 32 : at + 64])
        out_ref[dest, 256:288, :] = packed.astype(BF16)


def flat(ref):
    return jnp.concatenate([ref[at : at + 1, :] for at in range(COMPS // 128)], axis=1)


def prepare_sky(band_ref, dirs_ref, flux_ref, pol_ref, index_ref, clusters_ref, out_ref):
    ratio = 0.5 + 3.0 * (band_ref[0].astype(F32) + 0.5) / BANDS
    dir_l = dirs_ref[0:1, :]
    dir_m = dirs_ref[1:2, :]
    dir_n = jnp.sqrt(1.0 - dir_l * dir_l - dir_m * dir_m) - 1.0
    log_ratio = jnp.log(jnp.full((1, COMPS), ratio, F32))
    factor = jnp.exp(flat(index_ref) * log_ratio)
    flux = flat(flux_ref)
    stokes_q = pol_ref[0:1, :]
    rows = [
        dir_l * ratio,
        dir_m * ratio,
        dir_n * ratio,
        (flux + stokes_q) * factor,
        pol_ref[1:2, :] * factor,
        (flux - stokes_q) * factor,
    ]
    row_at = lax.broadcasted_iota(jnp.int32, (8, COMPS), 0)
    stacked = jnp.zeros((8, COMPS), F32)
    for at, row in enumerate(rows):
        stacked = jnp.where(row_at == at, row, stacked)
    high, middle, low = split3(stacked)
    table = jnp.concatenate(
        [high, high, high, middle, middle, low, jnp.zeros((80, COMPS), F32)], axis=0
    ).astype(BF16)
    clusters = flat(clusters_ref)
    hot = (lax.broadcasted_iota(jnp.int32, (16, COMPS), 0) == clusters).astype(F32)
    before = (
        lax.broadcasted_iota(jnp.int32, (128, 128), 0)
        < lax.broadcasted_iota(jnp.int32, (128, 128), 1)
    ).astype(BF16)
    seen = jnp.zeros((16, 1), F32)
    ranks = []
    for at in range(COMPS // 128):
        part = hot[:, at * 128 : at * 128 + 128]
        inside = jnp.dot(part.astype(BF16), before, preferred_element_type=F32) + seen
        ranks.append(jnp.sum(inside * part, axis=0, keepdims=True))
        seen = seen + jnp.sum(part, axis=1, keepdims=True)
    place = 16 * jnp.concatenate(ranks, axis=1).astype(jnp.int32) + clusters
    for at in range(COMPS // 256):
        target = lax.broadcasted_iota(jnp.int32, (256, COMPS), 0) + at * 256
        chosen = (target == place).astype(F32).astype(BF16)
        out_ref[at * 256 : at * 256 + 256, :] = lax.dot_general(
            chosen, table, (((1,), (1,)), ((), ())), preferred_element_type=F32
        ).astype(BF16)


def station_operand(rows8):
    high, middle, low = split3(rows8)
    width = rows8.shape[1]
    return jnp.concatenate(
        [high, middle, low, high, middle, high, jnp.zeros((80, width), F32)], axis=0
    ).astype(BF16)


def model_kernel(
    sky_ref, all_ref, own_ref, far_ref, weighted_ref, model_ref, geo_ref, geo_own_ref, gains_ref
):
    step = pl.program_id(0)
    lower = lax.broadcasted_iota(jnp.int32, (1, 128), 1) < 64

    @pl.when(step == 0)
    def _():
        model_ref[...] = jnp.zeros_like(model_ref)
        geo_own_ref[...] = station_operand(own_ref[64:72, :])
        for tile in range(8):
            first, second = all_ref[2 * tile], all_ref[2 * tile + 1]
            lanes = slice(tile * 128, tile * 128 + 128)
            geo_ref[:, lanes] = station_operand(jnp.where(lower, first[64:72], second[64:72]))
            low_part = jnp.where(lower, first[0:64], pltpu.roll(second[0:64], 64, 1))
            high_part = jnp.where(lower, pltpu.roll(first[0:64], 64, 1), second[0:64])
            gains_ref[:, lanes] = low_part
            gains_ref[:, 1024 + tile * 128 : 1024 + tile * 128 + 128] = high_part

    sky = sky_ref[...]
    own_re, own_im = phases(jnp.dot(sky, geo_own_ref[...], preferred_element_type=F32))
    source = lax.broadcasted_iota(jnp.int32, (128, 384), 0)
    target = 3 + lax.broadcasted_iota(jnp.int32, (128, 384), 1) // 128
    select = (source == target) | (source == target + 24) | (source == target + 40)
    weights = jnp.dot(sky, select.astype(F32).astype(BF16), preferred_element_type=F32)
    weighted = []
    for flux in range(3):
        weight = weights[:, flux * 128 : flux * 128 + 128]
        pair = ((own_re * weight).astype(BF16), (own_im * weight).astype(BF16))
        weighted_ref[2 * flux] = pair[0]
        weighted_ref[2 * flux + 1] = pair[1]
        weighted.append((pair[0].astype(F32), pair[1].astype(F32)))
    gains = [jnp.concatenate([own_ref[at * 16 : at * 16 + 16]] * (SPAN // 16), axis=0) for at in range(4)]
    near_re, near_im = [], []
    for first, second in ((0, 1), (1, 2)):
        (ar, ai), (br, bi) = weighted[first], weighted[second]
        real = gains[0] * ar - gains[1] * ai + gains[2] * br - gains[3] * bi
        imag = gains[0] * ai + gains[1] * ar + gains[2] * bi + gains[3] * br
        near_re.append(real.T)
        near_im.append(imag.T)
    near = jnp.concatenate(
        [
            jnp.concatenate(near_re + near_im, axis=1),
            jnp.concatenate(near_im + [-near_re[0], -near_re[1]], axis=1),
        ],
        axis=0,
    ).astype(BF16)
    for lane in range(0, NS, CHUNK):
        turns = jnp.dot(
            sky, geo_ref[:, lane : lane + CHUNK], preferred_element_type=F32
        )
        for at in range(0, SPAN, 16):
            rows = slice(at, at + 16)
            real, imag = phases(turns[rows])
            for row in range(2):
                lanes = slice(row * NS + lane, row * NS + lane + CHUNK)
                for column in range(2):
                    gain_re = gains_ref[column * 32 : column * 32 + 16, lanes]
                    gain_im = gains_ref[column * 32 + 16 : column * 32 + 32, lanes]
                    far_ref[column, rows, lanes] = (real * gain_re - imag * gain_im).astype(BF16)
                    far_ref[2 + column, rows, lanes] = (real * gain_im + imag * gain_re).astype(
                        BF16
                    )
        for row in range(2):
            lanes = slice(row * NS + lane, row * NS + lane + CHUNK)
            far = far_ref[:, :, lanes].reshape(4 * SPAN, CHUNK)
            model_ref[:, lanes] += jnp.dot(near, far, preferred_element_type=F32)


def gradient_kernel(
    band_ref,
    block_ref,
    far_ref,
    weighted_ref,
    vis_ref,
    mask_ref,
    got_ref,
    model_ref,
    own_ref,
    duals_ref,
    consensus_ref,
    drive_ref,
    square_ref,
    both_ref,
    near_ref,
    sum_ref,
    turned_ref,
):
    step = pl.program_id(0)
    own_tile = block_ref[0] // 2

    @pl.when(step == 0)
    def _():
        sum_ref[...] = jnp.zeros_like(sum_ref)
        lower = lax.broadcasted_iota(jnp.int32, (1, 128), 1) < 64

        def both_sides(tile, lane):
            lanes = pl.ds(lane, 128)
            far_lanes = pl.ds(NS + lane, 128)
            mask = mask_ref[:, lanes].astype(F32)

            def halves(top, count):
                first = got_ref[2 * tile, top : top + count, :].astype(F32)
                second = got_ref[2 * tile + 1, top : top + count, :].astype(F32)
                return (
                    jnp.where(lower, first, pltpu.roll(second, 64, 1)),
                    jnp.where(lower, pltpu.roll(first, 64, 1), second),
                )

            mask_both = mask + jnp.concatenate(halves(256, 32), axis=0)
            for row in range(2):
                for column in range(2):
                    real, imag = halves((2 * column + row) * 64, 64)
                    for part, other in ((0, real), (1, -imag)):
                        top = part * 128 + row * 64
                        vis = vis_ref[4 * row + 2 * column + part, :, lanes]
                        model = model_ref[top : top + 64, far_lanes if column else lanes]
                        yield top, column, vis * mask + other - mask_both * model

        for tile in range(8):
            for top, column, value in both_sides(tile, tile * 128):
                at = column * NS + tile * 128
                both_ref[top : top + 64, at : at + 128] = value.astype(BF16)
        for top, column, value in both_sides(own_tile, pl.multiple_of(own_tile * 128, 128)):
            near_ref[top : top + 64, column * 128 : column * 128 + 128] = (
                value - value.astype(BF16).astype(F32)
            ).astype(BF16)
        for lane in range(0, 2 * NS, 256):
            turned_ref[lane : lane + 256, :] = both_ref[:, lane : lane + 256].T

    product = jnp.dot(
        far_ref[...].reshape(4 * SPAN, 2 * NS), turned_ref[...], preferred_element_type=F32
    )
    lane = pl.multiple_of(own_tile * 128, 128)
    beside = jnp.concatenate(
        [
            far_ref[:, :, pl.ds(lane, 128)].reshape(4 * SPAN, 128),
            far_ref[:, :, pl.ds(NS + lane, 128)].reshape(4 * SPAN, 128),
        ],
        axis=1,
    )
    product = product + lax.dot_general(
        beside, near_ref[...], (((1,), (1,)), ((), ())), preferred_element_type=F32
    )
    terms = []
    for column in range(2):
        real_rows = product[column * SPAN : column * SPAN + SPAN]
        imag_rows = product[(2 + column) * SPAN : (2 + column) * SPAN + SPAN]
        terms.append(
            (
                real_rows[:, :128] - imag_rows[:, 128:],
                imag_rows[:, :128] + real_rows[:, 128:],
            )
        )
    weighted = [weighted_ref[at].astype(F32) for at in range(6)]
    for column, (first, second) in enumerate(((0, 1), (1, 2))):
        real = jnp.zeros((SPAN, 128), F32)
        imag = jnp.zeros((SPAN, 128), F32)
        for (tr, ti), flux in zip(terms, (first, second)):
            wr, wi = weighted[2 * flux], weighted[2 * flux + 1]
            real = real + (tr * wr + ti * wi)
            imag = imag + (ti * wr - tr * wi)
        for part, value in enumerate((real, imag)):
            at = (2 * column + part) * 16
            sum_ref[at : at + 16] += jnp.sum(value.reshape(SPAN // 16, 16, 128), axis=0)

    @pl.when(step == STEPS - 1)
    def _():
        basis = band_basis(band_ref[0])
        poly = jnp.zeros((64, 128), F32)
        for at in range(4):
            poly = poly + basis[at] * gains_rows(consensus_ref, (at,))
        penalty = PENALTY / 2.0 * (own_ref[0:64, :] - poly + gains_rows(duals_ref))
        drive = penalty - sum_ref[...]
        drive_ref[...] = drive
        square_ref[...] = jnp.broadcast_to(
            jnp.sum(drive * drive, axis=0, keepdims=True), square_ref.shape
        )


def update_kernel(squares_ref, drive_ref, own_ref, duals_ref, next_ref, shared_ref):
    total = jnp.sum(squares_ref[...], axis=(0, 1), keepdims=True)
    length = STEP_SIZE / jnp.sqrt(total / ENTRIES + 1e-6)
    rows = own_ref[0:64, :] - length * drive_ref[...]
    put_gains(next_ref, rows)
    shared_ref[...] = jnp.broadcast_to((rows + gains_rows(duals_ref))[None], shared_ref.shape)


def finish_kernel(band_ref, shared_ref, own_ref, duals_ref, consensus_ref):
    table = legendre_rows()
    gram = table.T @ table
    lower = np.linalg.cholesky(gram)
    sums = []
    for at in range(4):
        total = shared_ref[0] * float(table[0, at])
        for band in range(1, BANDS):
            total = total + shared_ref[band] * float(table[band, at])
        sums.append(total)
    forward = []
    for row in range(4):
        current = sums[row]
        for col in range(row):
            current = current - float(lower[row, col]) * forward[col]
        forward.append(current * float(1.0 / lower[row, row]))
    backward = [None] * 4
    for row in (3, 2, 1, 0):
        current = forward[row]
        for col in range(row + 1, 4):
            current = current - float(lower[col, row]) * backward[col]
        backward[row] = current * float(1.0 / lower[row, row])
    basis = band_basis(band_ref[0])
    poly = jnp.zeros((64, 128), F32)
    for at in range(4):
        put_gains(consensus_ref, backward[at], (at,))
        poly = poly + basis[at] * backward[at]
    put_gains(duals_ref, own_ref[0] - poly)


def cost(flops, moved):
    return pl.CostEstimate(flops=int(flops), bytes_accessed=int(moved), transcendentals=0)


BIG = pltpu.CompilerParams(vmem_limit_bytes=54 * 1024 * 1024)
shape = jax.ShapeDtypeStruct


def call_model(sky, everyone, own):
    return pl.pallas_call(
        model_kernel,
        grid=(STEPS,),
        in_specs=[
            pl.BlockSpec((SPAN, 128), lambda at: (at, 0)),
            VMEM,
            VMEM,
        ],
        out_specs=[
            pl.BlockSpec((4, SPAN, 2 * NS), lambda at: (0, at, 0)),
            pl.BlockSpec((6, SPAN, 128), lambda at: (0, at, 0)),
            pl.BlockSpec((256, 2 * NS), lambda at: (0, 0)),
        ],
        out_shape=[
            shape((4, COMPS, 2 * NS), BF16),
            shape((6, COMPS, 128), BF16),
            shape((256, 2 * NS), F32),
        ],
        scratch_shapes=[
            pltpu.VMEM((128, NS), BF16),
            pltpu.VMEM((128, 128), BF16),
            pltpu.VMEM((64, 2 * NS), F32),
        ],
        compiler_params=BIG,
        cost_estimate=cost(2e10, 4e7),
        name="model",
    )(sky, everyone, own)


def call_gradient(*operands):
    return pl.pallas_call(
        gradient_kernel,
        grid=(STEPS,),
        in_specs=[
            SMEM,
            SMEM,
            pl.BlockSpec((4, SPAN, 2 * NS), lambda at: (0, at, 0)),
            pl.BlockSpec((6, SPAN, 128), lambda at: (0, at, 0)),
        ]
        + [VMEM] * 7,
        out_specs=[VMEM, VMEM],
        out_shape=[shape((64, 128), F32), shape((BLOCKS, 128), F32)],
        scratch_shapes=[
            pltpu.VMEM((256, 2 * NS), BF16),
            pltpu.VMEM((256, 256), BF16),
            pltpu.VMEM((64, 128), F32),
            pltpu.VMEM((2 * NS, 256), BF16),
        ],
        compiler_params=BIG,
        cost_estimate=cost(7e9, 3e7),
        name="gradient",
    )(*operands)


def local(
    visibilities,
    flag_mask,
    stations,
    directions,
    intensity,
    polarized,
    spectral,
    clusters,
    jones_gains,
    scaled_duals,
    consensus,
):
    band = lax.axis_index("freq").reshape(1).astype(jnp.int32)
    block = lax.axis_index("stn").reshape(1).astype(jnp.int32)
    vis, jones, duals = visibilities[0], jones_gains[0], scaled_duals[0]
    own, copies = pl.pallas_call(
        packet_kernel,
        out_shape=[shape((72, 128), F32), shape((BLOCKS, 72, 128), F32)],
        in_specs=[VMEM] * 2,
        out_specs=[VMEM, VMEM],
        name="packet",
    )(jones, stations)
    everyone = lax.all_to_all(copies, "stn", 0, 0, tiled=True)
    outgoing, sky = pl.pallas_call(
        prepare_kernel,
        grid=(8,),
        in_specs=[
            SMEM,
            pl.BlockSpec((8, OWN, 128), lambda at: (0, 0, at)),
            pl.BlockSpec((OWN, 128), lambda at: (0, at)),
        ]
        + [VMEM] * 5,
        out_specs=[pl.BlockSpec((2, 288, 128), lambda at: (at, 0, 0)), VMEM],
        out_shape=[shape((BLOCKS, 288, 128), BF16), shape((COMPS, 128), BF16)],
        compiler_params=BIG,
        cost_estimate=cost(4e9, 1e6),
        name="prepare",
    )(
        band,
        vis,
        flag_mask,
        directions,
        intensity.reshape(COMPS // 128, 128),
        polarized,
        spectral.reshape(COMPS // 128, 128),
        clusters.reshape(COMPS // 128, 128),
    )
    incoming = lax.all_to_all(outgoing, "stn", 0, 0, tiled=True)
    incoming = pltpu.with_memory_space_constraint(incoming, pltpu.VMEM)
    far, weighted, model = call_model(sky, everyone, own)
    drive, squares = call_gradient(
        band,
        block,
        far,
        weighted,
        pltpu.with_memory_space_constraint(vis, pltpu.VMEM),
        pltpu.with_memory_space_constraint(flag_mask, pltpu.VMEM),
        incoming,
        model,
        own,
        duals,
        consensus,
    )
    squares = lax.all_to_all(squares, "stn", 0, 0, tiled=True)
    squares = pltpu.with_memory_space_constraint(squares, pltpu.VMEM)
    jones_next, shared = pl.pallas_call(
        update_kernel,
        out_shape=[shape((8, DIRS, OWN), F32), shape((BANDS, 64, 128), F32)],
        in_specs=[VMEM] * 4,
        out_specs=[VMEM, VMEM],
        name="update",
    )(squares, drive, own, duals)
    gathered = lax.all_to_all(shared, "freq", 0, 0, tiled=True)
    gathered = pltpu.with_memory_space_constraint(gathered, pltpu.VMEM)
    duals_next, consensus_next = pl.pallas_call(
        finish_kernel,
        grid=(1,),
        out_shape=[shape((8, DIRS, OWN), F32), shape((4, 8, DIRS, OWN), F32)],
        in_specs=[SMEM, VMEM, pl.BlockSpec((1, 64, 128), lambda at: (0, 0, 0))],
        out_specs=[VMEM, VMEM],
        name="finish",
    )(band, gathered, shared)
    return (jones_next[None], duals_next[None], consensus_next)


def solution(mesh):
    placed = (
        P("freq", None, "stn", None),
        P("stn", None),
        P(None, "stn"),
        P(),
        P(),
        P(),
        P(),
        P(),
        P("freq", None, None, "stn"),
        P("freq", None, None, "stn"),
        P(None, None, None, "stn"),
    )
    return jax.shard_map(
        local,
        mesh=mesh,
        in_specs=placed,
        out_specs=(
            P("freq", None, None, "stn"),
            P("freq", None, None, "stn"),
            P(None, None, None, "stn"),
        ),
        check_vma=False,
    )
```

```python
import math

import jax
import jax.numpy as jnp
import numpy as np
from jax import lax
from jax.experimental import pallas as pl
from jax.experimental.pallas import tpu as pltpu
from jax.sharding import PartitionSpec as P

DIRS = 16
COMPS = 1536
BANDS = 16
BLOCKS = 16
NS = 1024
OWN = 64
ENTRIES = 131072
PENALTY = 40.0
STEP_SIZE = 0.5
F32 = jnp.float32
BF16 = jnp.bfloat16
SPAN = 512
CHUNK = 256
STEPS = COMPS // SPAN
VMEM = pl.BlockSpec(memory_space=pltpu.VMEM)
SMEM = pl.BlockSpec(memory_space=pltpu.SMEM)


def turn_polynomials():
    nodes = (np.cos(np.pi * (np.arange(64) + 0.5) / 64) + 1.0) / 8.0
    root = np.sqrt(nodes)
    scale = np.sqrt(2.0)
    fits = []
    for values in (scale * np.cos(np.pi * root), -scale * np.sin(np.pi * root) / root):
        fit = np.polynomial.Chebyshev.fit(nodes, values, DEGREE, domain=[0, 0.25])
        fits.append([float(v) for v in fit.convert(kind=np.polynomial.Polynomial).coef])
    return fits


DEGREE = 3
COS_POLY, SIN_POLY = turn_polynomials()


def legendre_rows():
    centre = (2.0 * np.arange(BANDS) + 1.0) / BANDS - 1.0
    return np.stack(
        [
            np.ones_like(centre),
            centre,
            0.5 * (3.0 * centre * centre - 1.0),
            0.5 * (5.0 * centre * centre * centre - 3.0 * centre),
        ],
        axis=1,
    )


def horner(coefs, value):
    total = coefs[-1]
    for coef in coefs[-2::-1]:
        total = total * value + coef
    return total


def phases(turns):
    frac = turns - jnp.floor(turns + 0.5)
    square = frac * frac
    half_cos = horner(COS_POLY, square)
    half_sin = frac * horner(SIN_POLY, square)
    real = 1.0 - half_sin * half_sin
    imag = half_sin * half_cos
    return real.astype(BF16).astype(F32), imag.astype(BF16).astype(F32)


def split3(value):
    high = value.astype(BF16).astype(F32)
    rest = value - high
    middle = rest.astype(BF16).astype(F32)
    return high, middle, (rest - middle).astype(BF16).astype(F32)


def band_basis(band):
    centre = (2.0 * band.astype(F32) + 1.0) / BANDS - 1.0
    return (
        jnp.float32(1.0),
        centre,
        0.5 * (3.0 * centre * centre - 1.0),
        0.5 * (5.0 * centre * centre * centre - 3.0 * centre),
    )


def gains_rows(ref, lead=()):
    groups = []
    for column in range(2):
        for part in range(2):
            at = 2 * column + part
            groups.append(jnp.concatenate([ref[lead + (at,)], ref[lead + (4 + at,)]], axis=1))
    return jnp.concatenate(groups, axis=0)


def put_gains(ref, rows, lead=()):
    for column in range(2):
        for part in range(2):
            at = 2 * column + part
            group = rows[at * 16 : at * 16 + 16]
            ref[lead + (at,)] = group[:, :64]
            ref[lead + (4 + at,)] = group[:, 64:]


def packet_kernel(jones_ref, stations_ref, own_ref, copies_ref):
    place = jnp.concatenate([stations_ref[...], stations_ref[...]], axis=1)
    rows = jnp.concatenate([gains_rows(jones_ref), place, jnp.zeros((5, 128), F32)], axis=0)
    own_ref[...] = rows
    copies_ref[...] = jnp.broadcast_to(rows[None], copies_ref.shape)


def prepare_kernel(
    band_ref,
    vis_ref,
    mask_ref,
    dirs_ref,
    flux_ref,
    pol_ref,
    index_ref,
    clusters_ref,
    out_ref,
    sky_ref,
):
    @pl.when(pl.program_id(0) == 0)
    def _():
        prepare_sky(band_ref, dirs_ref, flux_ref, pol_ref, index_ref, clusters_ref, sky_ref)

    mask = mask_ref[...].astype(F32)

    def put(pair, real, imag):
        turned = jnp.concatenate([real, imag], axis=0).T.astype(BF16)
        for dest in range(2):
            out_ref[dest, pair * 64 : pair * 64 + 64, :] = turned[dest * 64 : dest * 64 + 64]

    for pair in range(4):
        put(pair, vis_ref[2 * pair] * mask, vis_ref[2 * pair + 1] * mask)
    lower = lax.broadcasted_iota(jnp.int32, (1, 128), 1) < 64
    turned = jnp.concatenate([mask, mask], axis=0).T
    for dest in range(2):
        at = dest * 64
        packed = jnp.where(lower, turned[at : at + 32], turned[at + 32 : at + 64])
        out_ref[dest, 256:288, :] = packed.astype(BF16)


def flat(ref):
    return jnp.concatenate([ref[at : at + 1, :] for at in range(COMPS // 128)], axis=1)


def prepare_sky(band_ref, dirs_ref, flux_ref, pol_ref, index_ref, clusters_ref, out_ref):
    ratio = 0.5 + 3.0 * (band_ref[0].astype(F32) + 0.5) / BANDS
    dir_l = dirs_ref[0:1, :]
    dir_m = dirs_ref[1:2, :]
    dir_n = jnp.sqrt(1.0 - dir_l * dir_l - dir_m * dir_m) - 1.0
    log_ratio = jnp.log(jnp.full((1, COMPS), ratio, F32))
    factor = jnp.exp(flat(index_ref) * log_ratio)
    flux = flat(flux_ref)
    stokes_q = pol_ref[0:1, :]
    rows = [
        dir_l * ratio,
        dir_m * ratio,
        dir_n * ratio,
        (flux + stokes_q) * factor,
        pol_ref[1:2, :] * factor,
        (flux - stokes_q) * factor,
    ]
    row_at = lax.broadcasted_iota(jnp.int32, (8, COMPS), 0)
    stacked = jnp.zeros((8, COMPS), F32)
    for at, row in enumerate(rows):
        stacked = jnp.where(row_at == at, row, stacked)
    high, middle, low = split3(stacked)
    table = jnp.concatenate(
        [high, high, high, middle, middle, low, jnp.zeros((80, COMPS), F32)], axis=0
    ).astype(BF16)
    clusters = flat(clusters_ref)
    hot = (lax.broadcasted_iota(jnp.int32, (16, COMPS), 0) == clusters).astype(F32)
    before = (
        lax.broadcasted_iota(jnp.int32, (128, 128), 0)
        < lax.broadcasted_iota(jnp.int32, (128, 128), 1)
    ).astype(BF16)
    seen = jnp.zeros((16, 1), F32)
    ranks = []
    for at in range(COMPS // 128):
        part = hot[:, at * 128 : at * 128 + 128]
        inside = jnp.dot(part.astype(BF16), before, preferred_element_type=F32) + seen
        ranks.append(jnp.sum(inside * part, axis=0, keepdims=True))
        seen = seen + jnp.sum(part, axis=1, keepdims=True)
    place = 16 * jnp.concatenate(ranks, axis=1).astype(jnp.int32) + clusters
    for at in range(COMPS // 256):
        target = lax.broadcasted_iota(jnp.int32, (256, COMPS), 0) + at * 256
        chosen = (target == place).astype(F32).astype(BF16)
        out_ref[at * 256 : at * 256 + 256, :] = lax.dot_general(
            chosen, table, (((1,), (1,)), ((), ())), preferred_element_type=F32
        ).astype(BF16)


def station_operand(rows8):
    high, middle, low = split3(rows8)
    width = rows8.shape[1]
    return jnp.concatenate(
        [high, middle, low, high, middle, high, jnp.zeros((80, width), F32)], axis=0
    ).astype(BF16)


def model_kernel(
    sky_ref, all_ref, own_ref, far_ref, weighted_ref, model_ref, geo_ref, geo_own_ref, gains_ref
):
    step = pl.program_id(0)
    lower = lax.broadcasted_iota(jnp.int32, (1, 128), 1) < 64

    @pl.when(step == 0)
    def _():
        model_ref[...] = jnp.zeros_like(model_ref)
        geo_own_ref[...] = station_operand(own_ref[64:72, :])
        for tile in range(8):
            first, second = all_ref[2 * tile], all_ref[2 * tile + 1]
            lanes = slice(tile * 128, tile * 128 + 128)
            geo_ref[:, lanes] = station_operand(jnp.where(lower, first[64:72], second[64:72]))
            low_part = jnp.where(lower, first[0:64], pltpu.roll(second[0:64], 64, 1))
            high_part = jnp.where(lower, pltpu.roll(first[0:64], 64, 1), second[0:64])
            gains_ref[:, lanes] = low_part
            gains_ref[:, 1024 + tile * 128 : 1024 + tile * 128 + 128] = high_part

    sky = sky_ref[...]
    own_re, own_im = phases(jnp.dot(sky, geo_own_ref[...], preferred_element_type=F32))
    source = lax.broadcasted_iota(jnp.int32, (128, 384), 0)
    target = 3 + lax.broadcasted_iota(jnp.int32, (128, 384), 1) // 128
    select = (source == target) | (source == target + 24) | (source == target + 40)
    weights = jnp.dot(sky, select.astype(F32).astype(BF16), preferred_element_type=F32)
    weighted = []
    for flux in range(3):
        weight = weights[:, flux * 128 : flux * 128 + 128]
        pair = ((own_re * weight).astype(BF16), (own_im * weight).astype(BF16))
        weighted_ref[2 * flux] = pair[0]
        weighted_ref[2 * flux + 1] = pair[1]
        weighted.append((pair[0].astype(F32), pair[1].astype(F32)))
    gains = [jnp.concatenate([own_ref[at * 16 : at * 16 + 16]] * (SPAN // 16), axis=0) for at in range(4)]
    near_re, near_im = [], []
    for first, second in ((0, 1), (1, 2)):
        (ar, ai), (br, bi) = weighted[first], weighted[second]
        real = gains[0] * ar - gains[1] * ai + gains[2] * br - gains[3] * bi
        imag = gains[0] * ai + gains[1] * ar + gains[2] * bi + gains[3] * br
        near_re.append(real.T)
        near_im.append(imag.T)
    near = jnp.concatenate(
        [
            jnp.concatenate(near_re + near_im, axis=1),
            jnp.concatenate(near_im + [-near_re[0], -near_re[1]], axis=1),
        ],
        axis=0,
    ).astype(BF16)
    for lane in range(0, NS, CHUNK):
        turns = jnp.dot(
            sky, geo_ref[:, lane : lane + CHUNK], preferred_element_type=F32
        )
        for at in range(0, SPAN, 16):
            rows = slice(at, at + 16)
            real, imag = phases(turns[rows])
            for row in range(2):
                lanes = slice(row * NS + lane, row * NS + lane + CHUNK)
                for column in range(2):
                    gain_re = gains_ref[column * 32 : column * 32 + 16, lanes]
                    gain_im = gains_ref[column * 32 + 16 : column * 32 + 32, lanes]
                    far_ref[column, rows, lanes] = (real * gain_re - imag * gain_im).astype(BF16)
                    far_ref[2 + column, rows, lanes] = (real * gain_im + imag * gain_re).astype(
                        BF16
                    )
        for row in range(2):
            lanes = slice(row * NS + lane, row * NS + lane + CHUNK)
            far = far_ref[:, :, lanes].reshape(4 * SPAN, CHUNK)
            model_ref[:, lanes] += jnp.dot(near, far, preferred_element_type=F32)


def gradient_kernel(
    band_ref,
    block_ref,
    far_ref,
    weighted_ref,
    vis_ref,
    mask_ref,
    got_ref,
    model_ref,
    own_ref,
    duals_ref,
    consensus_ref,
    drive_ref,
    square_ref,
    both_ref,
    near_ref,
    sum_ref,
    turned_ref,
):
    step = pl.program_id(0)
    own_tile = block_ref[0] // 2

    @pl.when(step == 0)
    def _():
        sum_ref[...] = jnp.zeros_like(sum_ref)
        lower = lax.broadcasted_iota(jnp.int32, (1, 128), 1) < 64

        def both_sides(tile, lane):
            lanes = pl.ds(lane, 128)
            far_lanes = pl.ds(NS + lane, 128)
            mask = mask_ref[:, lanes].astype(F32)

            def halves(top, count):
                first = got_ref[2 * tile, top : top + count, :].astype(F32)
                second = got_ref[2 * tile + 1, top : top + count, :].astype(F32)
                return (
                    jnp.where(lower, first, pltpu.roll(second, 64, 1)),
                    jnp.where(lower, pltpu.roll(first, 64, 1), second),
                )

            mask_both = mask + jnp.concatenate(halves(256, 32), axis=0)
            for row in range(2):
                for column in range(2):
                    real, imag = halves((2 * column + row) * 64, 64)
                    for part, other in ((0, real), (1, -imag)):
                        top = part * 128 + row * 64
                        vis = vis_ref[4 * row + 2 * column + part, :, lanes]
                        model = model_ref[top : top + 64, far_lanes if column else lanes]
                        yield top, column, vis * mask + other - mask_both * model

        for tile in range(8):
            for top, column, value in both_sides(tile, tile * 128):
                at = column * NS + tile * 128
                both_ref[top : top + 64, at : at + 128] = value.astype(BF16)
        for top, column, value in both_sides(own_tile, pl.multiple_of(own_tile * 128, 128)):
            near_ref[top : top + 64, column * 128 : column * 128 + 128] = (
                value - value.astype(BF16).astype(F32)
            ).astype(BF16)
        for lane in range(0, 2 * NS, 256):
            turned_ref[lane : lane + 256, :] = both_ref[:, lane : lane + 256].T

    product = jnp.dot(
        far_ref[...].reshape(4 * SPAN, 2 * NS), turned_ref[...], preferred_element_type=F32
    )
    lane = pl.multiple_of(own_tile * 128, 128)
    beside = jnp.concatenate(
        [
            far_ref[:, :, pl.ds(lane, 128)].reshape(4 * SPAN, 128),
            far_ref[:, :, pl.ds(NS + lane, 128)].reshape(4 * SPAN, 128),
        ],
        axis=1,
    )
    product = product + lax.dot_general(
        beside, near_ref[...], (((1,), (1,)), ((), ())), preferred_element_type=F32
    )
    terms = []
    for column in range(2):
        real_rows = product[column * SPAN : column * SPAN + SPAN]
        imag_rows = product[(2 + column) * SPAN : (2 + column) * SPAN + SPAN]
        terms.append(
            (
                real_rows[:, :128] - imag_rows[:, 128:],
                imag_rows[:, :128] + real_rows[:, 128:],
            )
        )
    weighted = [weighted_ref[at].astype(F32) for at in range(6)]
    for column, (first, second) in enumerate(((0, 1), (1, 2))):
        real = jnp.zeros((SPAN, 128), F32)
        imag = jnp.zeros((SPAN, 128), F32)
        for (tr, ti), flux in zip(terms, (first, second)):
            wr, wi = weighted[2 * flux], weighted[2 * flux + 1]
            real = real + (tr * wr + ti * wi)
            imag = imag + (ti * wr - tr * wi)
        for part, value in enumerate((real, imag)):
            at = (2 * column + part) * 16
            sum_ref[at : at + 16] += jnp.sum(value.reshape(SPAN // 16, 16, 128), axis=0)

    @pl.when(step == STEPS - 1)
    def _():
        basis = band_basis(band_ref[0])
        poly = jnp.zeros((64, 128), F32)
        for at in range(4):
            poly = poly + basis[at] * gains_rows(consensus_ref, (at,))
        penalty = PENALTY / 2.0 * (own_ref[0:64, :] - poly + gains_rows(duals_ref))
        drive = penalty - sum_ref[...]
        drive_ref[...] = drive
        square_ref[...] = jnp.broadcast_to(
            jnp.sum(drive * drive, axis=0, keepdims=True), square_ref.shape
        )


def update_kernel(squares_ref, drive_ref, own_ref, duals_ref, next_ref, shared_ref):
    total = jnp.sum(squares_ref[...], axis=(0, 1), keepdims=True)
    length = STEP_SIZE / jnp.sqrt(total / ENTRIES + 1e-6)
    rows = own_ref[0:64, :] - length * drive_ref[...]
    put_gains(next_ref, rows)
    shared_ref[...] = jnp.broadcast_to((rows + gains_rows(duals_ref))[None], shared_ref.shape)


def finish_kernel(band_ref, shared_ref, own_ref, duals_ref, consensus_ref):
    table = legendre_rows()
    gram = table.T @ table
    lower = np.linalg.cholesky(gram)
    sums = []
    for at in range(4):
        total = shared_ref[0] * float(table[0, at])
        for band in range(1, BANDS):
            total = total + shared_ref[band] * float(table[band, at])
        sums.append(total)
    forward = []
    for row in range(4):
        current = sums[row]
        for col in range(row):
            current = current - float(lower[row, col]) * forward[col]
        forward.append(current * float(1.0 / lower[row, row]))
    backward = [None] * 4
    for row in (3, 2, 1, 0):
        current = forward[row]
        for col in range(row + 1, 4):
            current = current - float(lower[col, row]) * backward[col]
        backward[row] = current * float(1.0 / lower[row, row])
    basis = band_basis(band_ref[0])
    poly = jnp.zeros((64, 128), F32)
    for at in range(4):
        put_gains(consensus_ref, backward[at], (at,))
        poly = poly + basis[at] * backward[at]
    put_gains(duals_ref, own_ref[0] - poly)


def cost(flops, moved):
    return pl.CostEstimate(flops=int(flops), bytes_accessed=int(moved), transcendentals=0)


BIG = pltpu.CompilerParams(vmem_limit_bytes=54 * 1024 * 1024)
shape = jax.ShapeDtypeStruct


def call_model(sky, everyone, own):
    return pl.pallas_call(
        model_kernel,
        grid=(STEPS,),
        in_specs=[
            pl.BlockSpec((SPAN, 128), lambda at: (at, 0)),
            VMEM,
            VMEM,
        ],
        out_specs=[
            pl.BlockSpec((4, SPAN, 2 * NS), lambda at: (0, at, 0)),
            pl.BlockSpec((6, SPAN, 128), lambda at: (0, at, 0)),
            pl.BlockSpec((256, 2 * NS), lambda at: (0, 0)),
        ],
        out_shape=[
            shape((4, COMPS, 2 * NS), BF16),
            shape((6, COMPS, 128), BF16),
            shape((256, 2 * NS), F32),
        ],
        scratch_shapes=[
            pltpu.VMEM((128, NS), BF16),
            pltpu.VMEM((128, 128), BF16),
            pltpu.VMEM((64, 2 * NS), F32),
        ],
        compiler_params=BIG,
        cost_estimate=cost(2e10, 4e7),
        name="model",
    )(sky, everyone, own)


def call_gradient(*operands):
    return pl.pallas_call(
        gradient_kernel,
        grid=(STEPS,),
        in_specs=[
            SMEM,
            SMEM,
            pl.BlockSpec((4, SPAN, 2 * NS), lambda at: (0, at, 0)),
            pl.BlockSpec((6, SPAN, 128), lambda at: (0, at, 0)),
        ]
        + [VMEM] * 7,
        out_specs=[VMEM, VMEM],
        out_shape=[shape((64, 128), F32), shape((BLOCKS, 128), F32)],
        scratch_shapes=[
            pltpu.VMEM((256, 2 * NS), BF16),
            pltpu.VMEM((256, 256), BF16),
            pltpu.VMEM((64, 128), F32),
            pltpu.VMEM((2 * NS, 256), BF16),
        ],
        compiler_params=BIG,
        cost_estimate=cost(7e9, 3e7),
        name="gradient",
    )(*operands)


def local(
    visibilities,
    flag_mask,
    stations,
    directions,
    intensity,
    polarized,
    spectral,
    clusters,
    jones_gains,
    scaled_duals,
    consensus,
):
    band = lax.axis_index("freq").reshape(1).astype(jnp.int32)
    block = lax.axis_index("stn").reshape(1).astype(jnp.int32)
    vis, jones, duals = visibilities[0], jones_gains[0], scaled_duals[0]
    own, copies = pl.pallas_call(
        packet_kernel,
        out_shape=[shape((72, 128), F32), shape((BLOCKS, 72, 128), F32)],
        in_specs=[VMEM] * 2,
        out_specs=[VMEM, VMEM],
        name="packet",
    )(jones, stations)
    everyone = lax.all_to_all(copies, "stn", 0, 0, tiled=True)
    outgoing, sky = pl.pallas_call(
        prepare_kernel,
        grid=(8,),
        in_specs=[
            SMEM,
            pl.BlockSpec((8, OWN, 128), lambda at: (0, 0, at)),
            pl.BlockSpec((OWN, 128), lambda at: (0, at)),
        ]
        + [VMEM] * 5,
        out_specs=[pl.BlockSpec((2, 288, 128), lambda at: (at, 0, 0)), VMEM],
        out_shape=[shape((BLOCKS, 288, 128), BF16), shape((COMPS, 128), BF16)],
        compiler_params=BIG,
        cost_estimate=cost(4e9, 1e6),
        name="prepare",
    )(
        band,
        vis,
        flag_mask,
        directions,
        intensity.reshape(COMPS // 128, 128),
        polarized,
        spectral.reshape(COMPS // 128, 128),
        clusters.reshape(COMPS // 128, 128),
    )
    incoming = lax.all_to_all(outgoing, "stn", 0, 0, tiled=True)
    incoming = pltpu.with_memory_space_constraint(incoming, pltpu.VMEM)
    far, weighted, model = call_model(sky, everyone, own)
    drive, squares = call_gradient(
        band,
        block,
        far,
        weighted,
        pltpu.with_memory_space_constraint(vis, pltpu.VMEM),
        pltpu.with_memory_space_constraint(flag_mask, pltpu.VMEM),
        incoming,
        model,
        own,
        duals,
        consensus,
    )
    squares = lax.all_to_all(squares, "stn", 0, 0, tiled=True)
    squares = pltpu.with_memory_space_constraint(squares, pltpu.VMEM)
    jones_next, shared = pl.pallas_call(
        update_kernel,
        out_shape=[shape((8, DIRS, OWN), F32), shape((BANDS, 64, 128), F32)],
        in_specs=[VMEM] * 4,
        out_specs=[VMEM, VMEM],
        name="update",
    )(squares, drive, own, duals)
    gathered = lax.all_to_all(shared, "freq", 0, 0, tiled=True)
    gathered = pltpu.with_memory_space_constraint(gathered, pltpu.VMEM)
    duals_next, consensus_next = pl.pallas_call(
        finish_kernel,
        grid=(1,),
        out_shape=[shape((8, DIRS, OWN), F32), shape((4, 8, DIRS, OWN), F32)],
        in_specs=[SMEM, VMEM, pl.BlockSpec((1, 64, 128), lambda at: (0, 0, 0))],
        out_specs=[VMEM, VMEM],
        name="finish",
    )(band, gathered, shared)
    return (jones_next[None], duals_next[None], consensus_next)


def solution(mesh):
    placed = (
        P("freq", None, "stn", None),
        P("stn", None),
        P(None, "stn"),
        P(),
        P(),
        P(),
        P(),
        P(),
        P("freq", None, None, "stn"),
        P("freq", None, None, "stn"),
        P(None, None, None, "stn"),
    )
    return jax.shard_map(
        local,
        mesh=mesh,
        in_specs=placed,
        out_specs=(
            P("freq", None, None, "stn"),
            P("freq", None, None, "stn"),
            P(None, None, None, "stn"),
        ),
        check_vma=False,
    )
```
